256 devices in a mesh: band: 64 (over x, z, core), mem: 4 (over y).
Axes of the slice: x: 4, y: 4, z: 8, core: 2. Of those that a mesh axis runs over, the one named last changes fastest.
Arguments:
- perturb: bfloat16 [80, 4, 256, 1536], P('mem', None, 'band'), may hold values from -0.8984375 to 0.8984375
- alpha_control: bfloat16 [80, 4, 256, 1536], P('mem', None, 'band'), may hold values from -6 to 6
- loc_factor: bfloat16 [1536, 1536], replicated
- static_control: bfloat16 [4, 1024, 4608], P(None, 'band'), may hold values from -6 to 6
- innovation: bfloat16 [4, 1024, 4608], P(None, 'band'), may hold values from -6 to 6
- obs_weight: bfloat16 [4, 1024, 4608], P(None, 'band'), may hold values from 0.099609375 to 1
- coarse_rows: int32 [64], replicated, may hold values from 2 to 4, as said below
- fine_rows: int32 [64], replicated, may hold values from 2 to 16, as said below
- source_row: int32 [1024], P('band'), may hold values from 0 to 190, as said below
- row_weight: float32 [1024], P('band'), may hold values from 0 to 1
Outputs:
- grad_alpha: bfloat16 [80, 4, 256, 1536], P('mem', None, 'band')
- grad_static: float32 [4, 1024, 4608], P(None, 'band')
The draws below stay inside these ranges and needn't reach their ends.
Inputs may be any that keep to these rules, and one draw needn't show every extreme that they name: `coarse_rows`: pairs of bands (2k, 2k+1) hold 3 + t and 3 - t rows with t in -1..1; the rows sum to 192. `fine_rows`: the fine rows sum to 576; the first fine row of band b lies within 2 of three times the first coarse row of band b. `source_row`: for a fine slot whose row index is j (slot s of band b stands for row first_f[b] + s, also past the band's live rows), the value is j // 3 or j // 3 - 1, clipped to 0 .. 190.
All inputs are finite; a program needn't handle non-finite values.
Results may differ from the reference program's by a relative error of at most 0.0029.
Values sent between devices are 32-bit elements; how exact they have to be, the bound alone decides.
No kernel may reach another device: no remote copies, remote signals or barrier semaphores. Data moves between devices by JAX's collectives and lax.ppermute only.
A program may use at most 64 MiB of HBM per device.

```python
import math
import jax
import jax.numpy as jnp
from jax import lax

MEMBERS = 80
LON_COARSE = 1536
LEVELS = 4
DIFF_STEPS = 2
COARSE_CAP = 4
BANDS = 64
LON_FINE = 4608
FINE_CAP = 16
COARSE_ROWS = 192
FINE_ROWS = 576
COARSE_SLOTS = 256
FINE_SLOTS = 1024


def band_layout(key):
    pair_key, jitter_key = jax.random.split(key)
    pair_moves = jax.random.randint(pair_key, (BANDS // 2,), -1, 2)
    pair_moves = pair_moves.at[0].set(1).at[1].set(1).at[2].set(-1)
    coarse = COARSE_CAP - 1 + jnp.stack([pair_moves, -pair_moves], axis=1).reshape(BANDS)
    offset = jax.random.randint(jitter_key, (BANDS + 1,), -2, 3)
    offset = offset.at[0].set(0).at[BANDS].set(0).at[2].set(-2).at[3].set(2).at[4].set(2).at[5].set(-2)
    first_rows = jnp.concatenate([jnp.zeros((1,), jnp.int32), jnp.cumsum(coarse).astype(jnp.int32)])
    fine_first = 3 * first_rows + offset
    return (coarse.astype(jnp.int32), (fine_first[1:] - fine_first[:-1]).astype(jnp.int32), fine_first.astype(jnp.int32))


def draw_coarse_rows(key, part):
    coarse, fine, fine_first = band_layout(key)
    return coarse


def draw_fine_rows(key, part):
    coarse, fine, fine_first = band_layout(key)
    return fine


def draw_source_row(key, part):
    coarse, fine, fine_first = band_layout(key)
    key = jax.random.fold_in(key, 7)
    slot_ids = jnp.arange(FINE_SLOTS, dtype=jnp.int32)
    owner_band = slot_ids // FINE_CAP
    row_ids = fine_first[owner_band] + slot_ids % FINE_CAP
    moves = jax.random.randint(key, (FINE_SLOTS,), -1, 1)
    return jnp.clip(row_ids // 3 + moves, 0, COARSE_ROWS - 2).astype(jnp.int32)


def draw_loc_factor(key, part):
    key = jax.random.fold_in(key, 11)
    columns = jnp.arange(LON_COARSE)
    distance = jnp.abs(columns[:, None] - columns[None, :])
    distance = jnp.minimum(distance, LON_COARSE - distance).astype(jnp.float32)
    random_part = jax.random.normal(key, (LON_COARSE, LON_COARSE), jnp.float32)
    spread_part = random_part * jnp.exp(-distance / (LON_COARSE / 8.0)) * (0.5 / jnp.sqrt(LON_COARSE / 8.0))
    return jnp.where(distance == 0.0, 1.0, spread_part).astype(jnp.bfloat16)


def block_levels(stream_key, extent, cuts, low, largest):
    factor_of = 1.0
    for position, parts in cuts:
        heights = jax.random.uniform(jax.random.fold_in(jax.random.fold_in(stream_key, 6), position), (parts,), jnp.float32, low / len(cuts), largest / len(cuts))
        factor_of = factor_of * jnp.repeat(jnp.exp(heights), extent[position] // parts).reshape((-1,) + (1,) * (len(extent) - 1 - position))
    return factor_of


def bell_draw(rng, extent, deviation, most, cuts=(), kind=jnp.bfloat16):
    loudness = block_levels(rng, extent, cuts, -0.22, 0.18) if cuts else 1.0
    entries = jax.random.normal(rng, extent, jnp.float32) * deviation * loudness
    return jnp.minimum(jnp.maximum(entries, -most), most).astype(kind)


def setup_inputs(seed: int = 0) -> dict:
    key_of = jax.random.split(jax.random.key(seed), 11)
    perturb = bell_draw(key_of[0], (MEMBERS, LEVELS, COARSE_SLOTS, LON_COARSE), 0.1125, 0.8984375, ((0, 4), (2, 64)))
    alpha_control = bell_draw(key_of[1], (MEMBERS, LEVELS, COARSE_SLOTS, LON_COARSE), 1.0, 6.0, ((0, 4), (2, 64)))
    loc_factor = draw_loc_factor(jax.random.fold_in(key_of[10], 71), 0)
    static_control = bell_draw(key_of[3], (LEVELS, FINE_SLOTS, LON_FINE), 1.0, 6.0, ((1, 64),))
    innovation = bell_draw(key_of[4], (LEVELS, FINE_SLOTS, LON_FINE), 1.0, 6.0, ((1, 64),))
    obs_weight = jnp.clip(jnp.exp(math.log(1.0) - 2.306499 * jax.random.uniform(key_of[5], (LEVELS, FINE_SLOTS, LON_FINE), jnp.float32) ** block_levels(key_of[5], (LEVELS, FINE_SLOTS, LON_FINE), ((1, 64),), -0.2, 0.2)), 0.099609375, 1.0).astype(jnp.bfloat16)
    coarse_rows = draw_coarse_rows(jax.random.fold_in(key_of[10], 71), 0)
    fine_rows = draw_fine_rows(jax.random.fold_in(key_of[10], 71), 0)
    source_row = draw_source_row(jax.random.fold_in(key_of[10], 71), 0)
    row_weight = jnp.clip(1.0 * jax.random.uniform(key_of[9], (FINE_SLOTS,), jnp.float32) ** block_levels(key_of[9], (FINE_SLOTS,), ((0, 64),), -0.2, 0.2), 0.0, 1.0)
    return dict(perturb=perturb, alpha_control=alpha_control, loc_factor=loc_factor, static_control=static_control, innovation=innovation, obs_weight=obs_weight, coarse_rows=coarse_rows, fine_rows=fine_rows, source_row=source_row, row_weight=row_weight)


diffusivity = 0.2

def refine_along(coarse):
    following = jnp.roll(coarse, -1, axis=-1)
    stacked = jnp.stack([coarse, (2.0 * coarse + following) / 3.0, (coarse + 2.0 * following) / 3.0], axis=-1)
    return stacked.reshape(coarse.shape[:-1] + (3 * coarse.shape[-1],))

def coarsen_along(gradient):
    split_up = gradient.reshape(gradient.shape[:-1] + (gradient.shape[-1] // 3, 3))
    own_part = split_up[..., 0] + split_up[..., 1] * (2.0 / 3.0) + split_up[..., 2] * (1.0 / 3.0)
    carried = split_up[..., 1] * (1.0 / 3.0) + split_up[..., 2] * (2.0 / 3.0)
    return own_part + jnp.roll(carried, 1, axis=-1)

def smooth_rows(values):
    zero_row = jnp.zeros_like(values[:, :1])
    upper_rows = jnp.concatenate([zero_row, values[:, :-1]], axis=1)
    lower_rows = jnp.concatenate([values[:, 1:], zero_row], axis=1)
    eastern = jnp.roll(values, -1, axis=2)
    western = jnp.roll(values, 1, axis=2)
    return values + diffusivity * (upper_rows + lower_rows + eastern + western - 4.0 * values)

def slot_layout(rows_per_band, capacity):
    first_rows = jnp.concatenate([jnp.zeros((1,), jnp.int32), jnp.cumsum(rows_per_band).astype(jnp.int32)])
    slot_ids = jnp.arange(rows_per_band.shape[0] * capacity, dtype=jnp.int32)
    owner_band = slot_ids // capacity
    offset_in = slot_ids % capacity
    latitude = first_rows[owner_band] + offset_in
    live_mask = offset_in < rows_per_band[owner_band]
    return (first_rows, latitude, live_mask)

def reference(perturb, alpha_control, loc_factor, static_control, innovation, obs_weight, coarse_rows, fine_rows, source_row, row_weight):
    first_c, lat_coarse, live_coarse = slot_layout(coarse_rows, COARSE_CAP)
    first_f, lat_fine, live_fine = slot_layout(fine_rows, FINE_CAP)
    fine_ids = jnp.arange(FINE_ROWS, dtype=jnp.int32)
    owner_band = lax.optimization_barrier(jnp.sum((first_f[1:][None, :] <= fine_ids[:, None]).astype(jnp.int32), axis=1))
    slot_of_row = (owner_band * FINE_CAP + fine_ids - first_f[owner_band]).astype(jnp.int32)
    coarse_live = live_coarse.astype(jnp.float32)
    fine_live = live_fine.astype(jnp.float32)

    def to_slots(compact):
        return jnp.take(compact, jnp.clip(lat_fine, 0, FINE_ROWS - 1), axis=1) * fine_live[None, :, None]

    def spread(values):
        compact = jnp.take(values, slot_of_row, axis=1)
        for number in range(DIFF_STEPS):
            compact = smooth_rows(compact)
        return to_slots(compact)

    def accumulate(running, members):
        perturb_one, alpha_one = members
        localized = jnp.dot(alpha_one.reshape(-1, LON_COARSE), loc_factor, preferred_element_type=jnp.float32).reshape(alpha_one.shape)
        return (running + perturb_one.astype(jnp.float32) * localized, None)
    increment, unused = lax.scan(accumulate, jnp.zeros((LEVELS, COARSE_SLOTS, LON_COARSE), jnp.float32), (perturb, alpha_control))
    hit_low = (lat_coarse[None, :] == source_row[:, None]).astype(jnp.float32)
    hit_high = (lat_coarse[None, :] == source_row[:, None] + 1).astype(jnp.float32)
    interp = fine_live[:, None] * coarse_live[None, :] * ((1.0 - row_weight)[:, None] * hit_low + row_weight[:, None] * hit_high)
    fine_band = jnp.einsum('jr,lrx->ljx', interp, increment, precision=lax.Precision.HIGHEST)
    ensemble = refine_along(fine_band)
    control = static_control.astype(jnp.float32) * fine_live[None, :, None]
    static_part = spread(control)
    residual = obs_weight.astype(jnp.float32) * (ensemble + static_part - innovation.astype(jnp.float32)) * fine_live[None, :, None]
    grad_static = (control + spread(residual)) * fine_live[None, :, None]
    back_band = coarsen_along(residual)
    coarse_back = jnp.einsum('jr,ljx->lrx', interp, back_band, precision=lax.Precision.HIGHEST)

    def member_grad(members):
        perturb_one, alpha_one = members
        schur_term = (perturb_one.astype(jnp.float32) * coarse_back).astype(jnp.bfloat16)
        pulled = lax.dot_general(schur_term.reshape(-1, LON_COARSE), loc_factor, (((1,), (1,)), ((), ())), preferred_element_type=jnp.float32).reshape(alpha_one.shape)
        return ((alpha_one.astype(jnp.float32) + pulled) * coarse_live[None, :, None]).astype(jnp.bfloat16)
    grad_alpha = lax.map(member_grad, (perturb, alpha_control))
    return (grad_alpha, grad_static)
```

```python
import jax
import jax.numpy as jnp
from jax import lax
from jax.experimental import pallas as pl
from jax.experimental.pallas import tpu as pltpu
from jax.sharding import PartitionSpec as P

F32 = jnp.float32
BF16 = jnp.bfloat16
THIRD = 1.0 / 3.0
VMEM = pl.BlockSpec(memory_space=pltpu.VMEM)
SMEM = pl.BlockSpec(memory_space=pltpu.SMEM)


def params(mib):
    return pltpu.CompilerParams(vmem_limit_bytes=mib << 20)


def same_chip(x):
    peers = lax.axis_size("band")
    return lax.ppermute(x, "band", [(i, i ^ 1) for i in range(peers)])


def cross_chip(x):
    peers = lax.axis_size("band")
    pairs = [(i, (i + 1) % peers) for i in range(1, peers, 2)]
    return lax.ppermute(x, "band", pairs + [(j, i) for i, j in pairs])


def mem_peer(x, by):
    peers = lax.axis_size("mem")
    return lax.ppermute(x, "mem", [(i, (i + by) % peers) for i in range(peers)])


def triple_table(width, transposed):
    rows = lax.broadcasted_iota(jnp.int32, (3 * width, 3 * width), 0)
    cols = lax.broadcasted_iota(jnp.int32, (3 * width, 3 * width), 1)
    if transposed:
        rows, cols = cols, rows
    return (rows == 3 * (cols % width) + cols // width).astype(BF16)


def lane_roll(x, by):
    return pltpu.roll(x, by % x.shape[-1], x.ndim - 1)


def smooth(planes, north, south):
    f0, f1, f2 = planes
    west0 = lane_roll(f2, 1)
    east2 = lane_roll(f0, -1)
    common = f0 + f1
    tail = f1 + f2
    return (
        0.2 * (common + west0 + (north[0] + south[0])),
        0.2 * (common + f2 + (north[1] + south[1])),
        0.2 * (tail + east2 + (north[2] + south[2])),
    )


def spread_level(own, first, last, below, above, live, row_ids, exists):
    top = row_ids == 0
    bottom = row_ids == live - 1
    count = own[0].shape[0]

    def shifted(v, lower, upper):
        north = [jnp.where(top, lo, pltpu.roll(x, 1, 0)) for x, lo in zip(v, lower)]
        south = [jnp.where(bottom, up, pltpu.roll(x, count - 1, 0)) for x, up in zip(v, upper)]
        return north, south

    edge = [b[1:2] for b in below]
    far = [b[0:1] for b in below]
    edge_below = [e * exists[0] for e in smooth(edge, far, first)]
    edge2 = [a[0:1] for a in above]
    far2 = [a[1:2] for a in above]
    edge_above = [e * exists[1] for e in smooth(edge2, last, far2)]
    once = smooth(own, *shifted(own, edge, edge2))
    return smooth(once, *shifted(once, edge_below, edge_above))


def localize_kernel(alpha_ref, perturb_ref, loc_ref, out_ref):
    members, levels, slots, count = alpha_ref.shape
    alpha = alpha_ref[...].reshape(members * levels * slots, count)
    localized = jnp.dot(alpha, loc_ref[...], preferred_element_type=F32)
    width = localized.shape[1]
    perturb = perturb_ref[...].astype(F32).reshape(members * levels * slots, width)
    out_ref[...] = jnp.sum((perturb * localized).reshape(members, levels * slots, width), axis=0)


def split_kernel(scalars_ref, control_ref, innovation_ref, weight_ref, control_out, innovation_out, weight_out, same_out, cross_out):
    own_fine, parity = scalars_ref[1], scalars_ref[3]
    levels, slots, count = control_ref.shape
    width = 128
    table = triple_table(width, False)
    live = (lax.broadcasted_iota(jnp.int32, (levels * slots, 1), 0) % slots < own_fine).astype(F32)
    for block in range(count // (3 * width)):
        span = slice(3 * width * block, 3 * width * (block + 1))
        stacked = jnp.concatenate(
            [r[:, :, span].reshape(levels * slots, 3 * width) for r in (control_ref, innovation_ref, weight_ref)], axis=0
        )
        planes = jnp.dot(stacked, table, preferred_element_type=F32)
        rows = levels * slots
        out = slice(width * block, width * (block + 1))
        for p in range(3):
            part = planes[:, p * width : (p + 1) * width]
            control_out[p, :, :, out] = (part[:rows] * live).reshape(levels, slots, width)
            innovation_out[p, :, :, out] = part[rows : 2 * rows].reshape(levels, slots, width).astype(BF16)
            weight_out[p, :, :, out] = (part[2 * rows :] * live).reshape(levels, slots, width).astype(BF16)
    same_start = jnp.where(parity == 0, own_fine - 2, 0)
    cross_start = jnp.where(parity == 0, 0, own_fine - 2)
    for p in range(3):
        for l in range(levels):
            at = (p * levels + l) * 2
            for k in range(2):
                same_out[at + k : at + k + 1, :] = control_out[p, l, pl.ds(same_start + k, 1), :]
                cross_out[at + k : at + k + 1, :] = control_out[p, l, pl.ds(cross_start + k, 1), :]


def neighbours(scalars_ref):
    device, bands = scalars_ref[2], scalars_ref[4]
    return (device > 0).astype(F32), (device < bands - 1).astype(F32)


def halo_rows(same_ref, cross_ref, scalars_ref, at):
    device, parity, bands = scalars_ref[2], scalars_ref[3], scalars_ref[4]
    same, cross = same_ref[at : at + 2, :], cross_ref[at : at + 2, :]
    below = jnp.where(parity == 0, cross, same) * (device > 0).astype(F32)
    above = jnp.where(parity == 0, same, cross) * (device < bands - 1).astype(F32)
    return below, above


def static_kernel(scalars_ref, control_ref, innovation_ref, same_ref, cross_ref, out_ref):
    own_fine = scalars_ref[1]
    planes, levels, slots, count = control_ref.shape
    row_ids = lax.broadcasted_iota(jnp.int32, (slots, 1), 0)
    exists = neighbours(scalars_ref)
    for l in range(levels):
        halos = [halo_rows(same_ref, cross_ref, scalars_ref, (p * levels + l) * 2) for p in range(3)]
        own = [control_ref[p, l] for p in range(3)]
        first = [control_ref[p, l, 0:1, :] for p in range(3)]
        last = [control_ref[p, l, pl.ds(own_fine - 1, 1), :] for p in range(3)]
        result = spread_level(own, first, last, [h[0] for h in halos], [h[1] for h in halos], own_fine, row_ids, exists)
        for p in range(3):
            out_ref[p, l] = result[p] - innovation_ref[p, l].astype(F32)


def increment_kernel(scalars_ref, own_ref, a_ref, b_ref, c_ref, total_ref, same_out, cross_out):
    own_coarse, parity = scalars_ref[0], scalars_ref[3]
    total_ref[...] = (own_ref[...] + a_ref[...]) + (b_ref[...] + c_ref[...])
    rows = total_ref.shape[0]
    same_start = jnp.where(parity == 0, own_coarse - 2, 0)
    cross_start = jnp.where(parity == 0, 0, own_coarse - 2)
    for l in range(rows // 4):
        for k in range(2):
            same_out[2 * l + k : 2 * l + k + 1, :] = total_ref[pl.ds(4 * l + same_start + k, 1), :]
            cross_out[2 * l + k : 2 * l + k + 1, :] = total_ref[pl.ds(4 * l + cross_start + k, 1), :]


def residual_kernel(
    scalars_ref, source_ref, upper_ref, total_ref, same_ref, cross_ref, static_ref, weight_ref,
    residual_out, back_out, same_out, cross_out, lower_scr, higher_scr,
):
    own_coarse, own_fine, device, parity, bands, first_row = (scalars_ref[i] for i in range(6))
    planes, levels, slots, count = static_ref.shape
    row_ids = lax.broadcasted_iota(jnp.int32, (slots, 1), 0)
    picked = lax.broadcasted_iota(jnp.int32, (slots, slots), 0) == lax.broadcasted_iota(jnp.int32, (slots, slots), 1)
    source = jnp.sum(jnp.where(picked, source_ref[...], 0), axis=1, keepdims=True)
    upper = jnp.sum(jnp.where(picked, upper_ref[...], 0.0), axis=1, keepdims=True)
    live = (row_ids < own_fine).astype(F32)
    low_weight, high_weight = live * (1.0 - upper), live * upper
    latitudes = [first_row - 2, first_row - 1] + [first_row + s for s in range(4)]
    latitudes += [first_row + own_coarse, first_row + own_coarse + 1]
    usable = [device > 0] * 2 + [s < own_coarse for s in range(4)] + [device < bands - 1] * 2
    coefficients = [
        (jnp.where(source == lat, low_weight, 0.0) + jnp.where(source + 1 == lat, high_weight, 0.0)) * ok.astype(F32)
        for lat, ok in zip(latitudes, usable)
    ]
    for l in range(levels):
        below, above = halo_rows(same_ref, cross_ref, scalars_ref, 2 * l)
        rows = [below[0:1], below[1:2]] + [total_ref[4 * l + s : 4 * l + s + 1, :] for s in range(4)]
        rows += [above[0:1], above[1:2]]
        band = coefficients[0] * rows[0]
        for c, r in zip(coefficients[1:], rows[1:]):
            band = band + c * r
        following = lane_roll(band, -1)
        fine = (band, (2.0 * band + following) * THIRD, (band + 2.0 * following) * THIRD)
        residual = []
        for p in range(3):
            value = weight_ref[p, l].astype(F32) * (fine[p] + static_ref[p, l])
            value = jnp.where(row_ids < own_fine, value, 0.0)
            residual_out[p, l] = value
            residual.append(value)
        g0, g1, g2 = residual
        back = (g0 + g1 * (2.0 * THIRD) + g2 * THIRD) + lane_roll(g1 * THIRD + g2 * (2.0 * THIRD), 1)
        sums = [jnp.sum(c * back, axis=0, keepdims=True) for c in coefficients]
        for s in range(4):
            back_out[4 * l + s : 4 * l + s + 1, :] = sums[2 + s]
        for k in range(2):
            lower_scr[2 * l + k : 2 * l + k + 1, :] = sums[k]
            higher_scr[2 * l + k : 2 * l + k + 1, :] = sums[6 + k]
    same_start = jnp.where(parity == 0, own_fine - 2, 0)
    cross_start = jnp.where(parity == 0, 0, own_fine - 2)
    for p in range(3):
        for l in range(levels):
            at = (p * levels + l) * 2
            for k in range(2):
                same_out[at + k : at + k + 1, :] = residual_out[p, l, pl.ds(same_start + k, 1), :]
                cross_out[at + k : at + k + 1, :] = residual_out[p, l, pl.ds(cross_start + k, 1), :]
    lower, higher = lower_scr[...], higher_scr[...]
    at = 3 * levels * 2
    same_out[at : at + 2 * levels, :] = jnp.where(parity == 0, higher, lower)
    cross_out[at : at + 2 * levels, :] = jnp.where(parity == 0, lower, higher)


def gradient_kernel(scalars_ref, back_ref, same_ref, cross_ref, alpha_ref, perturb_ref, loc_ref, out_ref, full_scr):
    own_coarse, device, parity, bands = scalars_ref[0], scalars_ref[2], scalars_ref[3], scalars_ref[4]
    members, levels, slots, count = perturb_ref.shape
    at = 3 * levels * 2
    same, cross = same_ref[at : at + 2 * levels, :], cross_ref[at : at + 2 * levels, :]
    below = jnp.where(parity == 0, cross, same) * (device > 0).astype(F32)
    above = jnp.where(parity == 0, same, cross) * (device < bands - 1).astype(F32)
    full_scr[...] = back_ref[...]
    for l in range(levels):
        full_scr[4 * l : 4 * l + 2, :] += below[2 * l : 2 * l + 2]
        for k in range(2):
            full_scr[pl.ds(4 * l + own_coarse - 2 + k, 1), :] += above[2 * l + k : 2 * l + k + 1]
    rows = members * levels * slots
    perturb = perturb_ref[...].astype(F32).reshape(members, levels * slots, count)
    schur = (perturb * full_scr[...][None]).astype(BF16).reshape(rows, count)
    pulled = lax.dot_general(schur, loc_ref[...], (((1,), (1,)), ((), ())), preferred_element_type=F32)
    width = pulled.shape[1]
    alpha = alpha_ref[...].astype(F32).reshape(rows, width)
    live = (lax.broadcasted_iota(jnp.int32, (rows, 1), 0) % slots < own_coarse).astype(F32)
    out_ref[...] = ((alpha + pulled) * live).reshape(members, levels, slots, width).astype(BF16)


def final_kernel(scalars_ref, control_ref, residual_ref, same_ref, cross_ref, out_ref, grad_scr):
    own_fine = scalars_ref[1]
    planes, levels, slots, count = control_ref.shape
    row_ids = lax.broadcasted_iota(jnp.int32, (slots, 1), 0)
    exists = neighbours(scalars_ref)
    for l in range(levels):
        halos = [halo_rows(same_ref, cross_ref, scalars_ref, (p * levels + l) * 2) for p in range(3)]
        own = [residual_ref[p, l] for p in range(3)]
        first = [residual_ref[p, l, 0:1, :] for p in range(3)]
        last = [residual_ref[p, l, pl.ds(own_fine - 1, 1), :] for p in range(3)]
        result = spread_level(own, first, last, [h[0] for h in halos], [h[1] for h in halos], own_fine, row_ids, exists)
        for p in range(3):
            grad_scr[p, l] = jnp.where(row_ids < own_fine, control_ref[p, l] + result[p], 0.0)
    width = 128
    table = triple_table(width, True)
    for block in range(count // width):
        span = slice(width * block, width * (block + 1))
        joined = jnp.concatenate([grad_scr[p, :, :, span].reshape(levels * slots, width) for p in range(3)], axis=1)
        high = joined.astype(BF16)
        low = (joined - high.astype(F32)).astype(BF16)
        mixed = jnp.dot(high, table, preferred_element_type=F32) + jnp.dot(low, table, preferred_element_type=F32)
        out_ref[:, :, 3 * width * block : 3 * width * (block + 1)] = mixed.reshape(levels, slots, 3 * width)


def on_device(
    perturb, alpha_control, loc_factor, static_control, innovation, obs_weight, coarse_rows, fine_rows, source_row, row_weight
):
    device = lax.axis_index("band")
    bands = lax.axis_size("band")
    members, levels, slots, count = perturb.shape
    fine_slots = static_control.shape[1]
    here = jnp.arange(bands, dtype=jnp.int32)
    counts = jnp.stack([
        jnp.sum(jnp.where(here == device, coarse_rows, 0)),
        jnp.sum(jnp.where(here == device, fine_rows, 0)),
        device,
        device % 2,
        jnp.int32(bands),
        jnp.sum(jnp.where(here < device, coarse_rows, 0)),
    ]).astype(jnp.int32)
    rows = levels * slots
    chunk = 256
    steps = count // chunk

    partial = pl.pallas_call(
        localize_kernel,
        out_shape=jax.ShapeDtypeStruct((rows, count), F32),
        grid=(steps,),
        in_specs=[
            pl.BlockSpec((members, levels, slots, count), lambda i: (0, 0, 0, 0)),
            pl.BlockSpec((members, levels, slots, chunk), lambda i: (0, 0, 0, i)),
            pl.BlockSpec((count, chunk), lambda i: (0, i)),
        ],
        out_specs=pl.BlockSpec((rows, chunk), lambda i: (0, i)),
        compiler_params=params(24),
    )(alpha_control, perturb, loc_factor)
    peers = [mem_peer(partial, by) for by in (1, 2, 3)]

    plane = (3, levels, fine_slots, count)
    wide = jax.ShapeDtypeStruct((6 * levels, count), F32)
    control, innovation_planes, weight_planes, control_same, control_cross = pl.pallas_call(
        split_kernel,
        out_shape=(
            jax.ShapeDtypeStruct(plane, F32), jax.ShapeDtypeStruct(plane, BF16), jax.ShapeDtypeStruct(plane, BF16), wide, wide
        ),
        in_specs=[SMEM, VMEM, VMEM, VMEM],
        out_specs=(VMEM,) * 5,
        compiler_params=params(24),
    )(counts, static_control, innovation, obs_weight)
    control_from_same = same_chip(control_same)
    control_from_cross = cross_chip(control_cross)
    static_minus = pl.pallas_call(
        static_kernel,
        out_shape=jax.ShapeDtypeStruct(plane, F32),
        in_specs=[SMEM, VMEM, VMEM, VMEM, VMEM],
        out_specs=VMEM,
        compiler_params=params(24),
    )(counts, control, innovation_planes, control_from_same, control_from_cross)

    pair = jax.ShapeDtypeStruct((2 * levels, count), F32)
    total, total_same, total_cross = pl.pallas_call(
        increment_kernel,
        out_shape=(jax.ShapeDtypeStruct((rows, count), F32), pair, pair),
        in_specs=[SMEM] + [VMEM] * 4,
        out_specs=(VMEM,) * 3,
        compiler_params=params(24),
    )(counts, partial, *peers)
    total_from_same = same_chip(total_same)
    total_from_cross = cross_chip(total_cross)

    outgoing = jax.ShapeDtypeStruct((8 * levels, count), F32)
    residual, back, residual_same, residual_cross = pl.pallas_call(
        residual_kernel,
        out_shape=(jax.ShapeDtypeStruct(plane, F32), jax.ShapeDtypeStruct((rows, count), F32), outgoing, outgoing),
        in_specs=[SMEM] + [VMEM] * 7,
        out_specs=(VMEM,) * 4,
        scratch_shapes=[pltpu.VMEM((2 * levels, count), F32), pltpu.VMEM((2 * levels, count), F32)],
        compiler_params=params(24),
    )(
        counts, source_row.reshape(1, fine_slots), row_weight.reshape(1, fine_slots), total, total_from_same, total_from_cross,
        static_minus, weight_planes,
    )
    from_same = same_chip(residual_same)
    from_cross = cross_chip(residual_cross)

    grad_alpha = pl.pallas_call(
        gradient_kernel,
        out_shape=jax.ShapeDtypeStruct(perturb.shape, BF16),
        grid=(steps,),
        in_specs=[
            SMEM,
            pl.BlockSpec((rows, count), lambda i: (0, 0)),
            pl.BlockSpec((8 * levels, count), lambda i: (0, 0)),
            pl.BlockSpec((8 * levels, count), lambda i: (0, 0)),
            pl.BlockSpec((members, levels, slots, chunk), lambda i: (0, 0, 0, i)),
            pl.BlockSpec((members, levels, slots, count), lambda i: (0, 0, 0, 0)),
            pl.BlockSpec((chunk, count), lambda i: (i, 0)),
        ],
        out_specs=pl.BlockSpec((members, levels, slots, chunk), lambda i: (0, 0, 0, i)),
        scratch_shapes=[pltpu.VMEM((rows, count), F32)],
        compiler_params=params(24),
    )(counts, back, from_same, from_cross, alpha_control, perturb, loc_factor)

    grad_static = pl.pallas_call(
        final_kernel,
        out_shape=jax.ShapeDtypeStruct(static_control.shape, F32),
        in_specs=[SMEM] + [VMEM] * 4,
        out_specs=VMEM,
        scratch_shapes=[pltpu.VMEM(plane, F32)],
        compiler_params=params(24),
    )(counts, control, residual, from_same, from_cross)
    return (grad_alpha, grad_static)


def solution(mesh):
    placed = (
        P("mem", None, "band", None),
        P("mem", None, "band", None),
        P(),
        P(None, "band", None),
        P(None, "band", None),
        P(None, "band", None),
        P(),
        P(),
        P("band"),
        P("band"),
    )
    return jax.shard_map(
        on_device,
        mesh=mesh,
        in_specs=placed,
        out_specs=(P("mem", None, "band", None), P(None, "band", None)),
        check_vma=False,
    )
```

```python
import jax
import jax.numpy as jnp
from jax import lax
from jax.experimental import pallas as pl
from jax.experimental.pallas import tpu as pltpu
from jax.sharding import PartitionSpec as P

F32 = jnp.float32
BF16 = jnp.bfloat16
THIRD = 1.0 / 3.0
VMEM = pl.BlockSpec(memory_space=pltpu.VMEM)
SMEM = pl.BlockSpec(memory_space=pltpu.SMEM)
HBM = pl.BlockSpec(memory_space=pltpu.HBM)


def params(mib):
    return pltpu.CompilerParams(vmem_limit_bytes=mib << 20)


def same_chip(x):
    peers = lax.axis_size("band")
    return lax.ppermute(x, "band", [(i, i ^ 1) for i in range(peers)])


def cross_chip(x):
    bands, mems = lax.axis_size("band"), lax.axis_size("mem")
    pairs = []
    for m in range(mems):
        pairs += [(i * mems + m, (i + 1) * mems + m) for i in range(1, bands - 1, 2)]
        pairs += [((i + 1) * mems + m, i * mems + m) for i in range(1, bands - 1, 2)]
        pairs += [(i * mems + m, i * mems + (m ^ 1)) for i in (0, bands - 1)]
    return lax.ppermute(x, ("band", "mem"), pairs)


def mem_peer(x, by):
    peers = lax.axis_size("mem")
    return lax.ppermute(x, "mem", [(i, (i + by) % peers) for i in range(peers)])


def triple_table(width, transposed):
    rows = lax.broadcasted_iota(jnp.int32, (3 * width, 3 * width), 0)
    cols = lax.broadcasted_iota(jnp.int32, (3 * width, 3 * width), 1)
    if transposed:
        rows, cols = cols, rows
    return (rows == 3 * (cols % width) + cols // width).astype(BF16)


def lane_roll(x, by):
    return pltpu.roll(x, by % x.shape[-1], x.ndim - 1)


def smooth(planes, north, south):
    f0, f1, f2 = planes
    west0 = lane_roll(f2, 1)
    east2 = lane_roll(f0, -1)
    common = f0 + f1
    tail = f1 + f2
    return (
        0.2 * (common + west0 + (north[0] + south[0])),
        0.2 * (common + f2 + (north[1] + south[1])),
        0.2 * (tail + east2 + (north[2] + south[2])),
    )


def spread_own(own, first, last, live, row_ids, exists):
    top = row_ids == 0
    bottom = row_ids == live - 1
    count = own[0].shape[0]

    def shifted(v, lower, upper):
        north = [jnp.where(top, lo, pltpu.roll(x, 1, 0)) for x, lo in zip(v, lower)]
        south = [jnp.where(bottom, up, pltpu.roll(x, count - 1, 0)) for x, up in zip(v, upper)]
        return north, south

    zero = [0.0] * 3
    once = smooth(own, *shifted(own, zero, zero))
    below = [f * (0.2 * exists[0]) for f in first]
    above = [f * (0.2 * exists[1]) for f in last]
    return smooth(once, *shifted(once, below, above))


def spread_halo(rows, nearest):
    pair = lax.broadcasted_iota(jnp.int32, (rows[0].shape[0], 1), 0) % 2
    touching = [pltpu.roll(r, (r.shape[0] - 1) if nearest == 1 else 1, 0) for r in rows]
    t0, t1, t2 = touching
    spreads = (t0 + t1 + lane_roll(t2, 1), t0 + t1 + t2, t1 + t2 + lane_roll(t0, -1))
    return [0.04 * jnp.where(pair == 1 - nearest, 2.0 * s + r, r) for s, r in zip(spreads, rows)]


def neighbours(scalars_ref):
    device, bands = scalars_ref[2], scalars_ref[4]
    return (device > 0).astype(F32), (device < bands - 1).astype(F32)


def halo_rows(same_ref, cross_ref, scalars_ref, at, size):
    parity = scalars_ref[3]
    exists = neighbours(scalars_ref)
    same, cross = same_ref[at : at + size, :], cross_ref[at : at + size, :]
    return jnp.where(parity == 0, cross, same) * exists[0], jnp.where(parity == 0, same, cross) * exists[1]


def localize_kernel(alpha_ref, perturb_ref, loc_ref, out_ref, alpha_scr, perturb_scr, loc_scr, sems):
    members, levels, slots, count = alpha_ref.shape
    chunk = 512
    steps = count // chunk
    alpha_load = pltpu.make_async_copy(alpha_ref, alpha_scr, sems.at[0])
    perturb_load = pltpu.make_async_copy(perturb_ref, perturb_scr, sems.at[1])
    loads = []
    for c in range(steps):
        span = pl.ds(c * chunk, chunk)
        loads.append(pltpu.make_async_copy(loc_ref.at[:, span], loc_scr.at[:, span], sems.at[2 + c]))
    alpha_load.start()
    loads[0].start()
    loads[1].start()
    alpha_load.wait()
    perturb_load.start()
    alpha = alpha_scr[...].reshape(members * levels * slots, count)
    for c in range(steps):
        span = slice(c * chunk, (c + 1) * chunk)
        loads[c].wait()
        if c + 2 < steps:
            loads[c + 2].start()
        localized = jnp.dot(alpha, loc_scr[:, span], preferred_element_type=F32)
        if c == 0:
            perturb_load.wait()
        perturb = perturb_scr[:, :, :, span].astype(F32).reshape(members * levels * slots, chunk)
        out_ref[:, span] = jnp.sum((perturb * localized).reshape(members, levels * slots, chunk), axis=0)


def split_kernel(
    device_ref, coarse_ref, fine_ref, control_ref, innovation_ref, weight_ref,
    scalars_out, control_out, static_out, weight_out, same_out, cross_out, innovation_scr,
):
    bands = coarse_ref.shape[0]
    device = device_ref[0]
    parity = device % 2
    own_fine = fine_ref[device]
    scalars_out[0] = coarse_ref[device]
    scalars_out[1] = own_fine
    scalars_out[2] = device
    scalars_out[3] = parity
    scalars_out[4] = bands
    scalars_out[5] = 3 * (device - parity) + parity * coarse_ref[device - parity]
    levels, slots, count = control_ref.shape
    width = 128
    table = triple_table(width, False)
    rows = levels * slots
    live = (lax.broadcasted_iota(jnp.int32, (rows, 1), 0) % slots < own_fine).astype(F32)
    for block in range(count // (3 * width)):
        span = slice(3 * width * block, 3 * width * (block + 1))
        stacked = jnp.concatenate(
            [r[:, :, span].reshape(rows, 3 * width) for r in (control_ref, innovation_ref, weight_ref)], axis=0
        )
        planes = jnp.dot(stacked, table, preferred_element_type=F32)
        out = slice(width * block, width * (block + 1))
        for p in range(3):
            part = planes[:, p * width : (p + 1) * width]
            control_out[p, :, :, out] = (part[:rows] * live).reshape(levels, slots, width)
            innovation_scr[p, :, :, out] = part[rows : 2 * rows].reshape(levels, slots, width)
            weight_out[p, :, :, out] = (part[2 * rows :] * live).reshape(levels, slots, width).astype(BF16)
    same_start = jnp.where(parity == 0, own_fine - 2, 0)
    cross_start = jnp.where(parity == 0, 0, own_fine - 2)
    row_ids = lax.broadcasted_iota(jnp.int32, (slots, 1), 0)
    exists = (device > 0).astype(F32), (device < bands - 1).astype(F32)
    for l in range(levels):
        for p in range(3):
            at = (p * levels + l) * 2
            for k in range(2):
                same_out[at + k : at + k + 1, :] = control_out[p, l, pl.ds(same_start + k, 1), :]
                cross_out[at + k : at + k + 1, :] = control_out[p, l, pl.ds(cross_start + k, 1), :]
        own = [control_out[p, l] for p in range(3)]
        first = [control_out[p, l, 0:1, :] for p in range(3)]
        last = [control_out[p, l, pl.ds(own_fine - 1, 1), :] for p in range(3)]
        result = spread_own(own, first, last, own_fine, row_ids, exists)
        for p in range(3):
            static_out[p, l] = result[p] - innovation_scr[p, l]


def increment_kernel(scalars_ref, own_ref, a_ref, b_ref, c_ref, same_in, cross_in, total_ref, same_out, cross_out):
    own_coarse, parity = scalars_ref[0], scalars_ref[3]
    total_ref[...] = (own_ref[...] + a_ref[...]) + (b_ref[...] + c_ref[...])
    levels = total_ref.shape[0] // 4
    at = same_out.shape[0] - 2 * levels
    same_start = jnp.where(parity == 0, own_coarse - 2, 0)
    cross_start = jnp.where(parity == 0, 0, own_coarse - 2)
    for l in range(levels):
        for k in range(2):
            row = at + 2 * l + k
            same_out[row : row + 1, :] = total_ref[pl.ds(4 * l + same_start + k, 1), :]
            cross_out[row : row + 1, :] = total_ref[pl.ds(4 * l + cross_start + k, 1), :]


def residual_kernel(
    scalars_ref, source_ref, upper_ref, total_ref, same_ref, cross_ref, static_ref, weight_ref,
    residual_out, back_out, same_out, cross_out, lower_scr, higher_scr,
):
    own_coarse, own_fine, device, parity, bands, first_row = (scalars_ref[i] for i in range(6))
    planes, levels, slots, count = static_ref.shape
    size = 2 * levels
    row_ids = lax.broadcasted_iota(jnp.int32, (slots, 1), 0)
    picked = lax.broadcasted_iota(jnp.int32, (slots, slots), 0) == lax.broadcasted_iota(jnp.int32, (slots, slots), 1)
    source = jnp.sum(jnp.where(picked, source_ref[...], 0), axis=1, keepdims=True)
    upper = jnp.sum(jnp.where(picked, upper_ref[...], 0.0), axis=1, keepdims=True)
    live = (row_ids < own_fine).astype(F32)
    low_weight, high_weight = live * (1.0 - upper), live * upper
    latitudes = [first_row - 2, first_row - 1] + [first_row + s for s in range(4)]
    latitudes += [first_row + own_coarse, first_row + own_coarse + 1]
    usable = [device > 0] * 2 + [s < own_coarse for s in range(4)] + [device < bands - 1] * 2
    coefficients = [
        (jnp.where(source == lat, low_weight, 0.0) + jnp.where(source + 1 == lat, high_weight, 0.0)) * ok.astype(F32)
        for lat, ok in zip(latitudes, usable)
    ]
    halos = [halo_rows(same_ref, cross_ref, scalars_ref, p * size, size) for p in range(3)]
    static_below = spread_halo([h[0] for h in halos], 1)
    static_above = spread_halo([h[1] for h in halos], 0)
    edges = [row_ids == 0, row_ids == 1, row_ids == own_fine - 2, row_ids == own_fine - 1]
    row_below, row_above = halo_rows(same_ref, cross_ref, scalars_ref, 3 * size, size)
    for l in range(levels):
        at = 2 * l
        rows = [row_below[at : at + 1], row_below[at + 1 : at + 2]]
        rows += [total_ref[4 * l + s : 4 * l + s + 1, :] for s in range(4)]
        rows += [row_above[at : at + 1], row_above[at + 1 : at + 2]]
        band = coefficients[0] * rows[0]
        for c, r in zip(coefficients[1:], rows[1:]):
            band = band + c * r
        following = lane_roll(band, -1)
        fine = (band, (2.0 * band + following) * THIRD, (band + 2.0 * following) * THIRD)
        residual = []
        for p in range(3):
            lower, higher = static_below[p], static_above[p]
            low = jnp.where(edges[0], lower[at : at + 1], jnp.where(edges[1], lower[at + 1 : at + 2], 0.0))
            high = jnp.where(edges[2], higher[at : at + 1], jnp.where(edges[3], higher[at + 1 : at + 2], 0.0))
            value = weight_ref[p, l].astype(F32) * (fine[p] + (static_ref[p, l] + (low + high)))
            value = jnp.where(row_ids < own_fine, value, 0.0)
            residual_out[p, l] = value
            residual.append(value)
        g0, g1, g2 = residual
        back = (g0 + g1 * (2.0 * THIRD) + g2 * THIRD) + lane_roll(g1 * THIRD + g2 * (2.0 * THIRD), 1)
        sums = [jnp.sum(c * back, axis=0, keepdims=True) for c in coefficients]
        for s in range(4):
            back_out[4 * l + s : 4 * l + s + 1, :] = sums[2 + s]
        for k in range(2):
            lower_scr[at + k : at + k + 1, :] = sums[k]
            higher_scr[at + k : at + k + 1, :] = sums[6 + k]
    same_start = jnp.where(parity == 0, own_fine - 2, 0)
    cross_start = jnp.where(parity == 0, 0, own_fine - 2)
    for p in range(3):
        for l in range(levels):
            at = (p * levels + l) * 2
            for k in range(2):
                same_out[at + k : at + k + 1, :] = residual_out[p, l, pl.ds(same_start + k, 1), :]
                cross_out[at + k : at + k + 1, :] = residual_out[p, l, pl.ds(cross_start + k, 1), :]
    lower, higher = lower_scr[...], higher_scr[...]
    same_out[3 * size : 4 * size, :] = jnp.where(parity == 0, higher, lower)
    cross_out[3 * size : 4 * size, :] = jnp.where(parity == 0, lower, higher)


def join_planes(planes):
    width = 128
    rows, count = planes[0].shape
    blocks = count // width
    spans = [slice(width * block, width * (block + 1)) for block in range(blocks)]
    joined = jnp.concatenate([jnp.concatenate([p[:, span] for p in planes], axis=1) for span in spans], axis=0)
    high = joined.astype(BF16)
    low = (joined - high.astype(F32)).astype(BF16)
    both = jnp.dot(jnp.concatenate([high, low], axis=0), triple_table(width, True), preferred_element_type=F32)
    mixed = both[: blocks * rows] + both[blocks * rows :]
    return [mixed[block * rows : (block + 1) * rows] for block in range(blocks)]


def own_gradient_kernel(scalars_ref, control_ref, residual_ref, out_ref, grad_scr):
    own_fine = scalars_ref[1]
    planes, levels, slots, count = control_ref.shape
    row_ids = lax.broadcasted_iota(jnp.int32, (slots, 1), 0)
    exists = neighbours(scalars_ref)
    for l in range(levels):
        own = [residual_ref[p, l] for p in range(3)]
        first = [residual_ref[p, l, 0:1, :] for p in range(3)]
        last = [residual_ref[p, l, pl.ds(own_fine - 1, 1), :] for p in range(3)]
        result = spread_own(own, first, last, own_fine, row_ids, exists)
        for p in range(3):
            grad_scr[p, l] = jnp.where(row_ids < own_fine, control_ref[p, l] + result[p], 0.0)
    mixed = join_planes([grad_scr[p].reshape(levels * slots, count) for p in range(3)])
    for block, part in enumerate(mixed):
        out_ref[:, :, 384 * block : 384 * (block + 1)] = part.reshape(levels, slots, 384)


def gradient_kernel(
    scalars_ref, back_ref, same_ref, cross_ref, own_static_ref, alpha_ref, perturb_ref, loc_ref,
    alpha_out, static_out, full_scr, schur_scr, stage_scr, halo_scr, static_scr, sems,
):
    own_coarse, own_fine = scalars_ref[0], scalars_ref[1]
    members, levels, slots, count = perturb_ref.shape
    size = 2 * levels
    below, above = halo_rows(same_ref, cross_ref, scalars_ref, 3 * size, size)
    full_scr[...] = back_ref[...]
    for l in range(levels):
        full_scr[4 * l : 4 * l + 2, :] += below[2 * l : 2 * l + 2]
        for k in range(2):
            full_scr[pl.ds(4 * l + own_coarse - 2 + k, 1), :] += above[2 * l + k : 2 * l + k + 1]
    rows = members * levels * slots
    chunk = 256
    for c in range(count // chunk):
        span = slice(c * chunk, (c + 1) * chunk)
        perturb = perturb_ref[:, :, :, span].astype(F32).reshape(members, levels * slots, chunk)
        schur_scr[:, span] = (perturb * full_scr[:, span][None]).astype(BF16).reshape(rows, chunk)

    halos = [halo_rows(same_ref, cross_ref, scalars_ref, p * size, size) for p in range(3)]
    lower = spread_halo([h[0] for h in halos], 1)
    higher = spread_halo([h[1] for h in halos], 0)
    mixed = join_planes([jnp.concatenate([lower[p], higher[p]], axis=0) for p in range(3)])
    for block, part in enumerate(mixed):
        halo_scr[:, 384 * block : 384 * (block + 1)] = part
    static_scr[...] = own_static_ref[...]
    for l in range(levels):
        static_scr[l, 0:2, :] += halo_scr[2 * l : 2 * l + 2, :]
        for k in range(2):
            at = size + 2 * l + k
            static_scr[l, pl.ds(own_fine - 2 + k, 1), :] += halo_scr[at : at + 1, :]
    copies = [pltpu.make_async_copy(static_scr, static_out, sems.at[0])]
    copies[0].start()

    schur = schur_scr[...]
    live = (lax.broadcasted_iota(jnp.int32, (rows, 1), 0) % slots < own_coarse).astype(F32)
    for c in range(count // chunk):
        span = slice(c * chunk, (c + 1) * chunk)
        pulled = lax.dot_general(schur, loc_ref[span, :], (((1,), (1,)), ((), ())), preferred_element_type=F32)
        alpha = alpha_ref[:, :, :, span].astype(F32).reshape(rows, chunk)
        stage_scr[:, :, :, span] = ((alpha + pulled) * live).reshape(members, levels, slots, chunk).astype(BF16)
        copies.append(
            pltpu.make_async_copy(
                stage_scr.at[:, :, :, pl.ds(c * chunk, chunk)], alpha_out.at[:, :, :, pl.ds(c * chunk, chunk)], sems.at[1 + c]
            )
        )
        copies[-1].start()
    for copy in copies:
        copy.wait()


def on_device(
    perturb, alpha_control, loc_factor, static_control, innovation, obs_weight, coarse_rows, fine_rows, source_row, row_weight
):
    device = lax.axis_index("band").astype(jnp.int32).reshape(1)
    members, levels, slots, count = perturb.shape
    fine_slots = static_control.shape[1]
    rows = levels * slots
    steps = count // 256

    partial = pl.pallas_call(
        localize_kernel,
        out_shape=jax.ShapeDtypeStruct((rows, count), F32),
        in_specs=[HBM] * 3,
        out_specs=VMEM,
        scratch_shapes=[
            pltpu.VMEM(alpha_control.shape, BF16),
            pltpu.VMEM(perturb.shape, BF16),
            pltpu.VMEM(loc_factor.shape, BF16),
            pltpu.SemaphoreType.DMA((2 + count // 512,)),
        ],
        compiler_params=params(61),
    )(alpha_control, perturb, loc_factor)
    peers = [mem_peer(partial, by) for by in (1, 3, 2)]

    plane = (3, levels, fine_slots, count)
    outgoing = jax.ShapeDtypeStruct((8 * levels, count), F32)
    scalars, control, static_minus, weight_planes, same_send, cross_send = pl.pallas_call(
        split_kernel,
        out_shape=(
            jax.ShapeDtypeStruct((8,), jnp.int32),
            jax.ShapeDtypeStruct(plane, F32),
            jax.ShapeDtypeStruct(plane, F32),
            jax.ShapeDtypeStruct(plane, BF16),
            outgoing,
            outgoing,
        ),
        in_specs=[SMEM] * 3 + [VMEM] * 3,
        out_specs=(SMEM,) + (VMEM,) * 5,
        scratch_shapes=[pltpu.VMEM(plane, F32)],
        compiler_params=params(24),
    )(device, coarse_rows, fine_rows, static_control, innovation, obs_weight)

    total, same_send, cross_send = pl.pallas_call(
        increment_kernel,
        out_shape=(jax.ShapeDtypeStruct((rows, count), F32), outgoing, outgoing),
        in_specs=[SMEM] + [VMEM] * 6,
        out_specs=(VMEM,) * 3,
        input_output_aliases={5: 1, 6: 2},
        compiler_params=params(24),
    )(scalars, partial, *peers, same_send, cross_send)
    from_cross = cross_chip(cross_send)
    from_same = same_chip(same_send)

    residual, back, same_send, cross_send = pl.pallas_call(
        residual_kernel,
        out_shape=(jax.ShapeDtypeStruct(plane, F32), jax.ShapeDtypeStruct((rows, count), F32), outgoing, outgoing),
        in_specs=[SMEM] + [VMEM] * 7,
        out_specs=(VMEM,) * 4,
        scratch_shapes=[pltpu.VMEM((2 * levels, count), F32), pltpu.VMEM((2 * levels, count), F32)],
        compiler_params=params(24),
    )(
        scalars, source_row.reshape(1, fine_slots), row_weight.reshape(1, fine_slots), total, from_same, from_cross,
        static_minus, weight_planes,
    )
    from_cross = cross_chip(cross_send)
    from_same = same_chip(same_send)

    own_static = pl.pallas_call(
        own_gradient_kernel,
        out_shape=jax.ShapeDtypeStruct(static_control.shape, F32),
        in_specs=[SMEM] + [VMEM] * 2,
        out_specs=VMEM,
        scratch_shapes=[pltpu.VMEM(plane, F32)],
        compiler_params=params(24),
    )(scalars, control, residual)

    return pl.pallas_call(
        gradient_kernel,
        out_shape=(jax.ShapeDtypeStruct(perturb.shape, BF16), jax.ShapeDtypeStruct(static_control.shape, F32)),
        in_specs=[SMEM] + [VMEM] * 7,
        out_specs=(HBM, HBM),
        scratch_shapes=[
            pltpu.VMEM((rows, count), F32),
            pltpu.VMEM((members * rows, count), BF16),
            pltpu.VMEM(perturb.shape, BF16),
            pltpu.VMEM((rows, 3 * count), F32),
            pltpu.VMEM(static_control.shape, F32),
            pltpu.SemaphoreType.DMA((1 + steps,)),
        ],
        compiler_params=params(24),
    )(scalars, back, from_same, from_cross, own_static, alpha_control, perturb, loc_factor)


def solution(mesh):
    placed = (
        P("mem", None, "band", None),
        P("mem", None, "band", None),
        P(),
        P(None, "band", None),
        P(None, "band", None),
        P(None, "band", None),
        P(),
        P(),
        P("band"),
        P("band"),
    )
    return jax.shard_map(
        on_device,
        mesh=mesh,
        in_specs=placed,
        out_specs=(P("mem", None, "band", None), P(None, "band", None)),
        check_vma=False,
    )
```

```python
import jax
import jax.numpy as jnp
from jax import lax
from jax.experimental import pallas as pl
from jax.experimental.pallas import tpu as pltpu
from jax.sharding import PartitionSpec as P

F32 = jnp.float32
BF16 = jnp.bfloat16
THIRD = 1.0 / 3.0
VMEM = pl.BlockSpec(memory_space=pltpu.VMEM)
HBM = pl.BlockSpec(memory_space=pltpu.HBM)


def params(mib):
    return pltpu.CompilerParams(vmem_limit_bytes=mib << 20)


def same_chip(x):
    peers = lax.axis_size("band")
    return lax.ppermute(x, "band", [(i, i ^ 1) for i in range(peers)])


def cross_chip(x):
    bands, mems = lax.axis_size("band"), lax.axis_size("mem")
    pairs = []
    for m in range(mems):
        pairs += [(i * mems + m, (i + 1) * mems + m) for i in range(1, bands - 1, 2)]
        pairs += [((i + 1) * mems + m, i * mems + m) for i in range(1, bands - 1, 2)]
        pairs += [(i * mems + m, i * mems + (m ^ 1)) for i in (0, bands - 1)]
    return lax.ppermute(x, ("band", "mem"), pairs)


def mem_peer(x, by):
    peers = lax.axis_size("mem")
    return lax.ppermute(x, "mem", [(i, (i + by) % peers) for i in range(peers)])


def triple_table(width, transposed):
    rows = lax.broadcasted_iota(jnp.int32, (3 * width, 3 * width), 0)
    cols = lax.broadcasted_iota(jnp.int32, (3 * width, 3 * width), 1)
    if transposed:
        rows, cols = cols, rows
    return (rows == 3 * (cols % width) + cols // width).astype(BF16)


def lane_roll(x, by):
    return pltpu.roll(x, by % x.shape[-1], x.ndim - 1)


def smooth(planes, north, south):
    f0, f1, f2 = planes
    west0 = lane_roll(f2, 1)
    east2 = lane_roll(f0, -1)
    common = f0 + f1
    tail = f1 + f2
    return (
        0.2 * (common + west0 + (north[0] + south[0])),
        0.2 * (common + f2 + (north[1] + south[1])),
        0.2 * (tail + east2 + (north[2] + south[2])),
    )


def spread_own(own, first, last, live, row_ids, exists):
    top = row_ids == 0
    bottom = row_ids == live - 1
    count = own[0].shape[0]

    def shifted(v, lower, upper):
        north = [jnp.where(top, lo, pltpu.roll(x, 1, 0)) for x, lo in zip(v, lower)]
        south = [jnp.where(bottom, up, pltpu.roll(x, count - 1, 0)) for x, up in zip(v, upper)]
        return north, south

    zero = [0.0] * 3
    once = smooth(own, *shifted(own, zero, zero))
    below = [f * (0.2 * exists[0]) for f in first]
    above = [f * (0.2 * exists[1]) for f in last]
    return smooth(once, *shifted(once, below, above))


def spread_halo(rows, nearest):
    pair = lax.broadcasted_iota(jnp.int32, (rows[0].shape[0], 1), 0) % 2
    touching = [pltpu.roll(r, (r.shape[0] - 1) if nearest == 1 else 1, 0) for r in rows]
    t0, t1, t2 = touching
    spreads = (t0 + t1 + lane_roll(t2, 1), t0 + t1 + t2, t1 + t2 + lane_roll(t0, -1))
    return [0.04 * jnp.where(pair == 1 - nearest, 2.0 * s + r, r) for s, r in zip(spreads, rows)]


def neighbours(scalars_ref):
    device, bands = scalars_ref[2, 0], scalars_ref[4, 0]
    return (device > 0).astype(F32), (device < bands - 1).astype(F32)


def halo_rows(same_ref, cross_ref, scalars_ref, at, size):
    parity = scalars_ref[3, 0]
    exists = neighbours(scalars_ref)
    same, cross = same_ref[at : at + size, :], cross_ref[at : at + size, :]
    return jnp.where(parity == 0, cross, same) * exists[0], jnp.where(parity == 0, same, cross) * exists[1]


def localize_kernel(alpha_ref, perturb_ref, loc_ref, out_ref, alpha_scr, perturb_scr, loc_scr, sems):
    members, levels, slots, count = alpha_ref.shape
    chunk = 512
    steps = count // chunk
    alpha_load = pltpu.make_async_copy(alpha_ref, alpha_scr, sems.at[0])
    perturb_load = pltpu.make_async_copy(perturb_ref, perturb_scr, sems.at[1])
    loads = []
    for c in range(steps):
        span = pl.ds(c * chunk, chunk)
        loads.append(pltpu.make_async_copy(loc_ref.at[:, span], loc_scr.at[:, span], sems.at[2 + c]))
    alpha_load.start()
    loads[0].start()
    loads[1].start()
    alpha_load.wait()
    perturb_load.start()
    alpha = alpha_scr[...].reshape(members * levels * slots, count)
    for c in range(steps):
        span = slice(c * chunk, (c + 1) * chunk)
        loads[c].wait()
        if c + 2 < steps:
            loads[c + 2].start()
        localized = jnp.dot(alpha, loc_scr[:, span], preferred_element_type=F32)
        if c == 0:
            perturb_load.wait()
        perturb = perturb_scr[:, :, :, span].astype(F32).reshape(members * levels * slots, chunk)
        out_ref[:, span] = jnp.sum((perturb * localized).reshape(members, levels * slots, chunk), axis=0)


def split_kernel(
    device_ref, coarse_ref, fine_ref, control_ref, innovation_ref, weight_ref,
    scalars_out, control_out, static_out, weight_out, same_out, cross_out, innovation_scr,
):
    bands = coarse_ref.shape[1]
    device = device_ref[0, 0]
    parity = device % 2
    band_ids = lax.broadcasted_iota(jnp.int32, (1, bands), 1)
    own_coarse = jnp.sum(jnp.where(band_ids == device, coarse_ref[...], 0))
    own_fine = jnp.sum(jnp.where(band_ids == device, fine_ref[...], 0))
    first_row = 3 * (device - parity) + parity * (6 - own_coarse)
    for i, value in enumerate((own_coarse, own_fine, device, parity, bands, first_row)):
        scalars_out[i : i + 1, :] = jnp.full((1, scalars_out.shape[1]), value, jnp.int32)
    levels, slots, count = control_ref.shape
    width = 128
    table = triple_table(width, False)
    rows = levels * slots
    live = (lax.broadcasted_iota(jnp.int32, (rows, 1), 0) % slots < own_fine).astype(F32)
    blocks = count // (3 * width)
    stacked = [
        r[:, :, 3 * width * i : 3 * width * (i + 1)].reshape(rows, 3 * width)
        for r in (control_ref, innovation_ref, weight_ref)
        for i in range(blocks)
    ]
    planes = jnp.dot(jnp.concatenate(stacked, axis=0), table, preferred_element_type=F32)
    for i in range(blocks):
        out = slice(width * i, width * (i + 1))
        for p in range(3):
            control, innovation, weight = (
                planes[rows * (k * blocks + i) : rows * (k * blocks + i + 1), p * width : (p + 1) * width] for k in range(3)
            )
            control_out[p, :, :, out] = (control * live).reshape(levels, slots, width)
            innovation_scr[p, :, :, out] = innovation.reshape(levels, slots, width)
            weight_out[p, :, :, out] = (weight * live).reshape(levels, slots, width).astype(BF16)
    same_start = jnp.where(parity == 0, own_fine - 2, 0)
    cross_start = jnp.where(parity == 0, 0, own_fine - 2)
    row_ids = lax.broadcasted_iota(jnp.int32, (slots, 1), 0)
    exists = (device > 0).astype(F32), (device < bands - 1).astype(F32)
    for l in range(levels):
        for p in range(3):
            at = (p * levels + l) * 2
            for k in range(2):
                same_out[at + k : at + k + 1, :] = control_out[p, l, pl.ds(same_start + k, 1), :]
                cross_out[at + k : at + k + 1, :] = control_out[p, l, pl.ds(cross_start + k, 1), :]
        own = [control_out[p, l] for p in range(3)]
        first = [control_out[p, l, 0:1, :] for p in range(3)]
        last = [control_out[p, l, pl.ds(own_fine - 1, 1), :] for p in range(3)]
        result = spread_own(own, first, last, own_fine, row_ids, exists)
        for p in range(3):
            static_out[p, l] = result[p] - innovation_scr[p, l]


def static_edge_kernel(scalars_ref, cross_ref, same_ref, static_in, static_out):
    own_fine = scalars_ref[1, 0]
    planes, levels, slots, count = static_out.shape
    size = 2 * levels
    halos = [halo_rows(same_ref, cross_ref, scalars_ref, p * size, size) for p in range(3)]
    lower = spread_halo([h[0] for h in halos], 1)
    higher = spread_halo([h[1] for h in halos], 0)
    for p in range(3):
        for l in range(levels):
            static_out[p, l, 0:2, :] += lower[p][2 * l : 2 * l + 2]
            for k in range(2):
                static_out[p, l, pl.ds(own_fine - 2 + k, 1), :] += higher[p][2 * l + k : 2 * l + k + 1]


def increment_kernel(scalars_ref, own_ref, a_ref, b_ref, c_ref, total_ref, same_out, cross_out):
    own_coarse, parity = scalars_ref[0, 0], scalars_ref[3, 0]
    total_ref[...] = (own_ref[...] + a_ref[...]) + (b_ref[...] + c_ref[...])
    levels = total_ref.shape[0] // 4
    same_start = jnp.where(parity == 0, own_coarse - 2, 0)
    cross_start = jnp.where(parity == 0, 0, own_coarse - 2)
    for l in range(levels):
        for k in range(2):
            row = 2 * l + k
            same_out[row : row + 1, :] = total_ref[pl.ds(4 * l + same_start + k, 1), :]
            cross_out[row : row + 1, :] = total_ref[pl.ds(4 * l + cross_start + k, 1), :]


def halves(x):
    high = x.astype(BF16)
    return high, (x - high.astype(F32)).astype(BF16)


def residual_kernel(
    scalars_ref, source_ref, upper_ref, total_ref, cross_ref, same_ref, static_ref, weight_ref,
    residual_out, back_out, same_out, cross_out, lower_scr, higher_scr,
):
    own_coarse, own_fine, device, parity, bands, first_row = (scalars_ref[i, 0] for i in range(6))
    planes, levels, slots, count = static_ref.shape
    size = 2 * levels
    row_ids = lax.broadcasted_iota(jnp.int32, (slots, 1), 0)
    picked = lax.broadcasted_iota(jnp.int32, (slots, slots), 0) == lax.broadcasted_iota(jnp.int32, (slots, slots), 1)
    source = jnp.sum(jnp.where(picked, source_ref[...], 0), axis=1, keepdims=True)
    upper = jnp.sum(jnp.where(picked, upper_ref[...], 0.0), axis=1, keepdims=True)
    live = (row_ids < own_fine).astype(F32)
    low_weight, high_weight = live * (1.0 - upper), live * upper
    latitudes = [first_row - 2, first_row - 1] + [first_row + s for s in range(4)]
    latitudes += [first_row + own_coarse, first_row + own_coarse + 1]
    usable = [device > 0] * 2 + [s < own_coarse for s in range(4)] + [device < bands - 1] * 2
    coefficients = [
        (jnp.where(source == lat, low_weight, 0.0) + jnp.where(source + 1 == lat, high_weight, 0.0)) * ok.astype(F32)
        for lat, ok in zip(latitudes, usable)
    ]
    high_part, low_part = halves(jnp.concatenate(coefficients, axis=1))
    gather = jnp.concatenate([high_part, high_part, low_part], axis=0)
    row_below, row_above = halo_rows(same_ref, cross_ref, scalars_ref, 0, size)
    for l in range(levels):
        at = 2 * l
        rows = [row_below[at : at + 1], row_below[at + 1 : at + 2]]
        rows += [total_ref[4 * l + s : 4 * l + s + 1, :] for s in range(4)]
        rows += [row_above[at : at + 1], row_above[at + 1 : at + 2]]
        band = coefficients[0] * rows[0]
        for c, r in zip(coefficients[1:], rows[1:]):
            band = band + c * r
        following = lane_roll(band, -1)
        fine = (band, (2.0 * band + following) * THIRD, (band + 2.0 * following) * THIRD)
        residual = []
        for p in range(3):
            value = weight_ref[p, l].astype(F32) * (fine[p] + static_ref[p, l])
            value = jnp.where(row_ids < own_fine, value, 0.0)
            residual_out[p, l] = value
            residual.append(value)
        g0, g1, g2 = residual
        back = (g0 + g1 * (2.0 * THIRD) + g2 * THIRD) + lane_roll(g1 * THIRD + g2 * (2.0 * THIRD), 1)
        back_high, back_low = halves(back)
        stacked = jnp.concatenate([back_high, back_low, back_high], axis=0)
        sums = lax.dot_general(gather, stacked, (((0,), (0,)), ((), ())), preferred_element_type=F32)
        back_out[4 * l : 4 * l + 4, :] = sums[2:6]
        lower_scr[at : at + 2, :] = sums[0:2]
        higher_scr[at : at + 2, :] = sums[6:8]
    same_start = jnp.where(parity == 0, own_fine - 2, 0)
    cross_start = jnp.where(parity == 0, 0, own_fine - 2)
    for p in range(3):
        for l in range(levels):
            at = (p * levels + l) * 2
            for k in range(2):
                same_out[at + k : at + k + 1, :] = residual_out[p, l, pl.ds(same_start + k, 1), :]
                cross_out[at + k : at + k + 1, :] = residual_out[p, l, pl.ds(cross_start + k, 1), :]
    lower, higher = lower_scr[...], higher_scr[...]
    same_out[3 * size : 4 * size, :] = jnp.where(parity == 0, higher, lower)
    cross_out[3 * size : 4 * size, :] = jnp.where(parity == 0, lower, higher)


def join_planes(planes):
    width = 128
    rows, count = planes[0].shape
    blocks = count // width
    spans = [slice(width * block, width * (block + 1)) for block in range(blocks)]
    joined = jnp.concatenate([jnp.concatenate([p[:, span] for p in planes], axis=1) for span in spans], axis=0)
    high, low = halves(joined)
    both = jnp.dot(jnp.concatenate([high, low], axis=0), triple_table(width, True), preferred_element_type=F32)
    mixed = both[: blocks * rows] + both[blocks * rows :]
    return [mixed[block * rows : (block + 1) * rows] for block in range(blocks)]


def own_gradient_kernel(scalars_ref, control_ref, residual_ref, out_ref, grad_scr):
    own_fine = scalars_ref[1, 0]
    planes, levels, slots, count = control_ref.shape
    row_ids = lax.broadcasted_iota(jnp.int32, (slots, 1), 0)
    exists = neighbours(scalars_ref)
    for l in range(levels):
        own = [residual_ref[p, l] for p in range(3)]
        first = [residual_ref[p, l, 0:1, :] for p in range(3)]
        last = [residual_ref[p, l, pl.ds(own_fine - 1, 1), :] for p in range(3)]
        result = spread_own(own, first, last, own_fine, row_ids, exists)
        for p in range(3):
            grad_scr[p, l] = jnp.where(row_ids < own_fine, control_ref[p, l] + result[p], 0.0)
    mixed = join_planes([grad_scr[p].reshape(levels * slots, count) for p in range(3)])
    for block, part in enumerate(mixed):
        out_ref[:, :, 384 * block : 384 * (block + 1)] = part.reshape(levels, slots, 384)


def gradient_kernel(
    scalars_ref, back_ref, cross_ref, same_ref, own_static_ref, alpha_ref, perturb_ref, loc_ref,
    alpha_out, static_out, full_scr, schur_scr, stage_scr, halo_scr, static_scr, sems,
):
    own_coarse, own_fine = scalars_ref[0, 0], scalars_ref[1, 0]
    members, levels, slots, count = perturb_ref.shape
    size = 2 * levels
    below, above = halo_rows(same_ref, cross_ref, scalars_ref, 3 * size, size)
    full_scr[...] = back_ref[...]
    for l in range(levels):
        full_scr[4 * l : 4 * l + 2, :] += below[2 * l : 2 * l + 2]
        for k in range(2):
            full_scr[pl.ds(4 * l + own_coarse - 2 + k, 1), :] += above[2 * l + k : 2 * l + k + 1]
    rows = members * levels * slots
    chunk = 256
    for c in range(count // chunk):
        span = slice(c * chunk, (c + 1) * chunk)
        perturb = perturb_ref[:, :, :, span].astype(F32).reshape(members, levels * slots, chunk)
        schur_scr[:, span] = (perturb * full_scr[:, span][None]).astype(BF16).reshape(rows, chunk)

    halos = [halo_rows(same_ref, cross_ref, scalars_ref, p * size, size) for p in range(3)]
    lower = spread_halo([h[0] for h in halos], 1)
    higher = spread_halo([h[1] for h in halos], 0)
    mixed = join_planes([jnp.concatenate([lower[p], higher[p]], axis=0) for p in range(3)])
    for block, part in enumerate(mixed):
        halo_scr[:, 384 * block : 384 * (block + 1)] = part
    static_scr[...] = own_static_ref[...]
    for l in range(levels):
        static_scr[l, 0:2, :] += halo_scr[2 * l : 2 * l + 2, :]
        for k in range(2):
            at = size + 2 * l + k
            static_scr[l, pl.ds(own_fine - 2 + k, 1), :] += halo_scr[at : at + 1, :]
    copies = [pltpu.make_async_copy(static_scr, static_out, sems.at[0])]
    copies[0].start()

    schur = schur_scr[...]
    live = (lax.broadcasted_iota(jnp.int32, (rows, 1), 0) % slots < own_coarse).astype(F32)
    for c in range(count // chunk):
        span = slice(c * chunk, (c + 1) * chunk)
        pulled = lax.dot_general(schur, loc_ref[span, :], (((1,), (1,)), ((), ())), preferred_element_type=F32)
        alpha = alpha_ref[:, :, :, span].astype(F32).reshape(rows, chunk)
        stage_scr[:, :, :, span] = ((alpha + pulled) * live).reshape(members, levels, slots, chunk).astype(BF16)
        copies.append(
            pltpu.make_async_copy(
                stage_scr.at[:, :, :, pl.ds(c * chunk, chunk)], alpha_out.at[:, :, :, pl.ds(c * chunk, chunk)], sems.at[1 + c]
            )
        )
        copies[-1].start()
    for copy in copies:
        copy.wait()


def on_device(
    perturb, alpha_control, loc_factor, static_control, innovation, obs_weight, coarse_rows, fine_rows, source_row, row_weight
):
    device = lax.axis_index("band").astype(jnp.int32).reshape(1, 1)
    members, levels, slots, count = perturb.shape
    fine_slots = static_control.shape[1]
    rows = levels * slots
    steps = count // 256

    partial = pl.pallas_call(
        localize_kernel,
        out_shape=jax.ShapeDtypeStruct((rows, count), F32),
        in_specs=[HBM] * 3,
        out_specs=VMEM,
        scratch_shapes=[
            pltpu.VMEM(alpha_control.shape, BF16),
            pltpu.VMEM(perturb.shape, BF16),
            pltpu.VMEM(loc_factor.shape, BF16),
            pltpu.SemaphoreType.DMA((2 + count // 512,)),
        ],
        compiler_params=params(61),
    )(alpha_control, perturb, loc_factor)
    peers = [mem_peer(partial, by) for by in (1, 3, 2)]

    plane = (3, levels, fine_slots, count)
    outgoing = jax.ShapeDtypeStruct((8 * levels, count), F32)
    wide = jax.ShapeDtypeStruct((6 * levels, count), F32)
    scalars, control, static_minus, weight_planes, same_send, cross_send = pl.pallas_call(
        split_kernel,
        out_shape=(
            jax.ShapeDtypeStruct((8, 128), jnp.int32),
            jax.ShapeDtypeStruct(plane, F32),
            jax.ShapeDtypeStruct(plane, F32),
            jax.ShapeDtypeStruct(plane, BF16),
            wide,
            wide,
        ),
        in_specs=[VMEM] * 6,
        out_specs=(VMEM,) * 6,
        scratch_shapes=[pltpu.VMEM(plane, F32)],
        compiler_params=params(24),
    )(device, coarse_rows.reshape(1, -1), fine_rows.reshape(1, -1), static_control, innovation, obs_weight)

    static_from_cross = cross_chip(cross_send)
    static_from_same = same_chip(same_send)

    pair = jax.ShapeDtypeStruct((2 * levels, count), F32)
    total, same_send, cross_send = pl.pallas_call(
        increment_kernel,
        out_shape=(jax.ShapeDtypeStruct((rows, count), F32), pair, pair),
        in_specs=[VMEM] * 5,
        out_specs=(VMEM,) * 3,
        compiler_params=params(24),
    )(scalars, partial, *peers)
    from_cross = cross_chip(cross_send)
    from_same = same_chip(same_send)
    static_minus = pl.pallas_call(
        static_edge_kernel,
        out_shape=jax.ShapeDtypeStruct(plane, F32),
        in_specs=[VMEM] * 4,
        out_specs=VMEM,
        input_output_aliases={3: 0},
        compiler_params=params(24),
    )(scalars, static_from_cross, static_from_same, static_minus)

    residual, back, same_send, cross_send = pl.pallas_call(
        residual_kernel,
        out_shape=(jax.ShapeDtypeStruct(plane, F32), jax.ShapeDtypeStruct((rows, count), F32), outgoing, outgoing),
        in_specs=[VMEM] * 8,
        out_specs=(VMEM,) * 4,
        scratch_shapes=[pltpu.VMEM((2 * levels, count), F32), pltpu.VMEM((2 * levels, count), F32)],
        compiler_params=params(24),
    )(
        scalars, source_row.reshape(1, fine_slots), row_weight.reshape(1, fine_slots), total, from_cross, from_same,
        static_minus, weight_planes,
    )
    from_cross = cross_chip(cross_send)
    from_same = same_chip(same_send)

    own_static = pl.pallas_call(
        own_gradient_kernel,
        out_shape=jax.ShapeDtypeStruct(static_control.shape, F32),
        in_specs=[VMEM] * 3,
        out_specs=VMEM,
        scratch_shapes=[pltpu.VMEM(plane, F32)],
        compiler_params=params(24),
    )(scalars, control, residual)

    return pl.pallas_call(
        gradient_kernel,
        out_shape=(jax.ShapeDtypeStruct(perturb.shape, BF16), jax.ShapeDtypeStruct(static_control.shape, F32)),
        in_specs=[VMEM] * 8,
        out_specs=(HBM, HBM),
        scratch_shapes=[
            pltpu.VMEM((rows, count), F32),
            pltpu.VMEM((members * rows, count), BF16),
            pltpu.VMEM(perturb.shape, BF16),
            pltpu.VMEM((rows, 3 * count), F32),
            pltpu.VMEM(static_control.shape, F32),
            pltpu.SemaphoreType.DMA((1 + steps,)),
        ],
        compiler_params=params(24),
    )(scalars, back, from_cross, from_same, own_static, alpha_control, perturb, loc_factor)


def solution(mesh):
    placed = (
        P("mem", None, "band", None),
        P("mem", None, "band", None),
        P(),
        P(None, "band", None),
        P(None, "band", None),
        P(None, "band", None),
        P(),
        P(),
        P("band"),
        P("band"),
    )
    return jax.shard_map(
        on_device,
        mesh=mesh,
        in_specs=placed,
        out_specs=(P("mem", None, "band", None), P(None, "band", None)),
        check_vma=False,
    )
```

```python
import jax
import jax.numpy as jnp
from jax import lax
from jax.experimental import pallas as pl
from jax.experimental.pallas import tpu as pltpu
from jax.sharding import PartitionSpec as P

F32 = jnp.float32
BF16 = jnp.bfloat16
THIRD = 1.0 / 3.0
VMEM = pl.BlockSpec(memory_space=pltpu.VMEM)
HBM = pl.BlockSpec(memory_space=pltpu.HBM)


def params(mib):
    return pltpu.CompilerParams(vmem_limit_bytes=mib << 20)


def same_chip(x):
    peers = lax.axis_size("band")
    return lax.ppermute(x, "band", [(i, i ^ 1) for i in range(peers)])


def cross_chip(x):
    bands, mems = lax.axis_size("band"), lax.axis_size("mem")
    pairs = []
    for m in range(mems):
        pairs += [(i * mems + m, (i + 1) * mems + m) for i in range(1, bands - 1, 2)]
        pairs += [((i + 1) * mems + m, i * mems + m) for i in range(1, bands - 1, 2)]
        pairs += [(i * mems + m, i * mems + (m ^ 1)) for i in (0, bands - 1)]
    return lax.ppermute(x, ("band", "mem"), pairs)


def mem_peer(x, by):
    peers = lax.axis_size("mem")
    return lax.ppermute(x, "mem", [(i, (i + by) % peers) for i in range(peers)])


def triple_table(width, transposed):
    rows = lax.broadcasted_iota(jnp.int32, (3 * width, 3 * width), 0)
    cols = lax.broadcasted_iota(jnp.int32, (3 * width, 3 * width), 1)
    if transposed:
        rows, cols = cols, rows
    return (rows == 3 * (cols % width) + cols // width).astype(BF16)


def lane_roll(x, by):
    return pltpu.roll(x, by % x.shape[-1], x.ndim - 1)


def smooth(planes, north, south):
    f0, f1, f2 = planes
    west0 = lane_roll(f2, 1)
    east2 = lane_roll(f0, -1)
    common = f0 + f1
    tail = f1 + f2
    return (
        0.2 * (common + west0 + (north[0] + south[0])),
        0.2 * (common + f2 + (north[1] + south[1])),
        0.2 * (tail + east2 + (north[2] + south[2])),
    )


def spread_own(own, first, last, live, row_ids, exists):
    top = row_ids == 0
    bottom = row_ids == live - 1
    count = own[0].shape[0]

    def shifted(v, lower, upper):
        north = [jnp.where(top, lo, pltpu.roll(x, 1, 0)) for x, lo in zip(v, lower)]
        south = [jnp.where(bottom, up, pltpu.roll(x, count - 1, 0)) for x, up in zip(v, upper)]
        return north, south

    zero = [0.0] * 3
    once = smooth(own, *shifted(own, zero, zero))
    below = [f * (0.2 * exists[0]) for f in first]
    above = [f * (0.2 * exists[1]) for f in last]
    return smooth(once, *shifted(once, below, above))


def spread_halo(rows, nearest):
    pair = lax.broadcasted_iota(jnp.int32, (rows[0].shape[0], 1), 0) % 2
    touching = [pltpu.roll(r, (r.shape[0] - 1) if nearest == 1 else 1, 0) for r in rows]
    t0, t1, t2 = touching
    spreads = (t0 + t1 + lane_roll(t2, 1), t0 + t1 + t2, t1 + t2 + lane_roll(t0, -1))
    return [0.04 * jnp.where(pair == 1 - nearest, 2.0 * s + r, r) for s, r in zip(spreads, rows)]


def neighbours(scalars_ref):
    device, bands = scalars_ref[2, 0], scalars_ref[4, 0]
    return (device > 0).astype(F32), (device < bands - 1).astype(F32)


def halo_rows(same_ref, cross_ref, scalars_ref, at, size):
    parity = scalars_ref[3, 0]
    exists = neighbours(scalars_ref)
    same, cross = same_ref[at : at + size, :], cross_ref[at : at + size, :]
    return jnp.where(parity == 0, cross, same) * exists[0], jnp.where(parity == 0, same, cross) * exists[1]


def localize_kernel(alpha_ref, perturb_ref, loc_ref, out_ref, alpha_scr, perturb_scr, loc_scr, sems):
    members, levels, slots, count = alpha_ref.shape
    chunk = 512
    steps = count // chunk
    alpha_load = pltpu.make_async_copy(alpha_ref, alpha_scr, sems.at[0])
    perturb_load = pltpu.make_async_copy(perturb_ref, perturb_scr, sems.at[1])
    loads = []
    for c in range(steps):
        span = pl.ds(c * chunk, chunk)
        loads.append(pltpu.make_async_copy(loc_ref.at[:, span], loc_scr.at[:, span], sems.at[2 + c]))
    alpha_load.start()
    loads[0].start()
    loads[1].start()
    alpha_load.wait()
    perturb_load.start()
    alpha = alpha_scr[...].reshape(members * levels * slots, count)
    for c in range(steps):
        span = slice(c * chunk, (c + 1) * chunk)
        loads[c].wait()
        if c + 2 < steps:
            loads[c + 2].start()
        localized = jnp.dot(alpha, loc_scr[:, span], preferred_element_type=F32)
        if c == 0:
            perturb_load.wait()
        perturb = perturb_scr[:, :, :, span].astype(F32).reshape(members * levels * slots, chunk)
        out_ref[:, span] = jnp.sum((perturb * localized).reshape(members, levels * slots, chunk), axis=0)


def edges_kernel(device_ref, coarse_ref, fine_ref, control_ref, after_ref, scalars_out, same_out, cross_out):
    bands = coarse_ref.shape[1]
    device = device_ref[0, 0]
    parity = device % 2
    band_ids = lax.broadcasted_iota(jnp.int32, (1, bands), 1)
    own_coarse = jnp.sum(jnp.where(band_ids == device, coarse_ref[...], 0))
    own_fine = jnp.sum(jnp.where(band_ids == device, fine_ref[...], 0))
    first_row = 3 * (device - parity) + parity * (6 - own_coarse)
    for i, value in enumerate((own_coarse, own_fine, device, parity, bands, first_row)):
        scalars_out[i : i + 1, :] = jnp.full((1, scalars_out.shape[1]), value, jnp.int32)
    levels, slots, count = control_ref.shape
    same_start = jnp.where(parity == 0, own_fine - 2, 0)
    cross_start = jnp.where(parity == 0, 0, own_fine - 2)
    take = lax.broadcasted_iota(jnp.int32, (8, slots), 0)
    slot = lax.broadcasted_iota(jnp.int32, (8, slots), 1)
    wanted = jnp.where(take < 2, same_start + take, cross_start + take - 2)
    pick = ((slot == wanted) & (take < 4)).astype(BF16)
    width = 128
    blocks = count // (3 * width)
    rows = [jnp.dot(pick, control_ref[l], preferred_element_type=F32) for l in range(levels)]
    stacked = [rows[l][:, 3 * width * i : 3 * width * (i + 1)] for i in range(blocks) for l in range(levels)]
    stacked = jnp.concatenate(stacked, axis=0).astype(BF16)
    planes = jnp.dot(stacked, triple_table(width, False), preferred_element_type=F32)
    for i in range(blocks):
        out = slice(width * i, width * (i + 1))
        for l in range(levels):
            at = (i * levels + l) * 8
            for p in range(3):
                to = (p * levels + l) * 2
                same_out[to : to + 2, out] = planes[at : at + 2, p * width : (p + 1) * width]
                cross_out[to : to + 2, out] = planes[at + 2 : at + 4, p * width : (p + 1) * width]


def planes_kernel(scalars_ref, after_ref, control_ref, innovation_ref, weight_ref, control_out, innovation_out, weight_out):
    own_fine = scalars_ref[1, 0]
    levels, slots, count = control_ref.shape
    width = 128
    rows = levels * slots
    live = (lax.broadcasted_iota(jnp.int32, (rows, 1), 0) % slots < own_fine).astype(F32)
    blocks = count // (3 * width)
    stacked = [
        r[:, :, 3 * width * i : 3 * width * (i + 1)].reshape(rows, 3 * width)
        for r in (control_ref, innovation_ref, weight_ref)
        for i in range(blocks)
    ]
    planes = jnp.dot(jnp.concatenate(stacked, axis=0), triple_table(width, False), preferred_element_type=F32)
    for i in range(blocks):
        out = slice(width * i, width * (i + 1))
        for p in range(3):
            control, innovation, weight = (
                planes[rows * (k * blocks + i) : rows * (k * blocks + i + 1), p * width : (p + 1) * width] for k in range(3)
            )
            control_out[p, :, :, out] = (control * live).reshape(levels, slots, width)
            innovation_out[p, :, :, out] = innovation.reshape(levels, slots, width).astype(BF16)
            weight_out[p, :, :, out] = (weight * live).reshape(levels, slots, width).astype(BF16)


def static_kernel(scalars_ref, cross_ref, same_ref, control_ref, innovation_ref, static_out):
    own_fine = scalars_ref[1, 0]
    planes, levels, slots, count = control_ref.shape
    size = 2 * levels
    row_ids = lax.broadcasted_iota(jnp.int32, (slots, 1), 0)
    exists = neighbours(scalars_ref)
    halos = [halo_rows(same_ref, cross_ref, scalars_ref, p * size, size) for p in range(3)]
    lower = spread_halo([h[0] for h in halos], 1)
    higher = spread_halo([h[1] for h in halos], 0)
    for l in range(levels):
        own = [control_ref[p, l] for p in range(3)]
        first = [control_ref[p, l, 0:1, :] for p in range(3)]
        last = [control_ref[p, l, pl.ds(own_fine - 1, 1), :] for p in range(3)]
        result = spread_own(own, first, last, own_fine, row_ids, exists)
        for p in range(3):
            static_out[p, l] = result[p] - innovation_ref[p, l].astype(F32)
            static_out[p, l, 0:2, :] += lower[p][2 * l : 2 * l + 2]
            for k in range(2):
                static_out[p, l, pl.ds(own_fine - 2 + k, 1), :] += higher[p][2 * l + k : 2 * l + k + 1]


def increment_kernel(scalars_ref, own_ref, a_ref, b_ref, c_ref, total_ref, same_out, cross_out):
    own_coarse, parity = scalars_ref[0, 0], scalars_ref[3, 0]
    total_ref[...] = (own_ref[...] + a_ref[...]) + (b_ref[...] + c_ref[...])
    levels = total_ref.shape[0] // 4
    same_start = jnp.where(parity == 0, own_coarse - 2, 0)
    cross_start = jnp.where(parity == 0, 0, own_coarse - 2)
    for l in range(levels):
        for k in range(2):
            row = 2 * l + k
            same_out[row : row + 1, :] = total_ref[pl.ds(4 * l + same_start + k, 1), :]
            cross_out[row : row + 1, :] = total_ref[pl.ds(4 * l + cross_start + k, 1), :]


def halves(x):
    high = x.astype(BF16)
    return high, (x - high.astype(F32)).astype(BF16)


def residual_kernel(
    scalars_ref, source_ref, upper_ref, total_ref, cross_ref, same_ref, static_ref, weight_ref,
    residual_out, back_out, same_out, cross_out, lower_scr, higher_scr,
):
    own_coarse, own_fine, device, parity, bands, first_row = (scalars_ref[i, 0] for i in range(6))
    planes, levels, slots, count = static_ref.shape
    size = 2 * levels
    row_ids = lax.broadcasted_iota(jnp.int32, (slots, 1), 0)
    picked = lax.broadcasted_iota(jnp.int32, (slots, slots), 0) == lax.broadcasted_iota(jnp.int32, (slots, slots), 1)
    source = jnp.sum(jnp.where(picked, source_ref[...], 0), axis=1, keepdims=True)
    upper = jnp.sum(jnp.where(picked, upper_ref[...], 0.0), axis=1, keepdims=True)
    live = (row_ids < own_fine).astype(F32)
    low_weight, high_weight = live * (1.0 - upper), live * upper
    latitudes = [first_row - 2, first_row - 1] + [first_row + s for s in range(4)]
    latitudes += [first_row + own_coarse, first_row + own_coarse + 1]
    usable = [device > 0] * 2 + [s < own_coarse for s in range(4)] + [device < bands - 1] * 2
    coefficients = [
        (jnp.where(source == lat, low_weight, 0.0) + jnp.where(source + 1 == lat, high_weight, 0.0)) * ok.astype(F32)
        for lat, ok in zip(latitudes, usable)
    ]
    high_part, low_part = halves(jnp.concatenate(coefficients, axis=1))
    gather = jnp.concatenate([high_part, high_part, low_part], axis=0)
    row_below, row_above = halo_rows(same_ref, cross_ref, scalars_ref, 0, size)
    for l in range(levels):
        at = 2 * l
        rows = [row_below[at : at + 1], row_below[at + 1 : at + 2]]
        rows += [total_ref[4 * l + s : 4 * l + s + 1, :] for s in range(4)]
        rows += [row_above[at : at + 1], row_above[at + 1 : at + 2]]
        band = coefficients[0] * rows[0]
        for c, r in zip(coefficients[1:], rows[1:]):
            band = band + c * r
        following = lane_roll(band, -1)
        fine = (band, (2.0 * band + following) * THIRD, (band + 2.0 * following) * THIRD)
        residual = []
        for p in range(3):
            value = weight_ref[p, l].astype(F32) * (fine[p] + static_ref[p, l])
            value = jnp.where(row_ids < own_fine, value, 0.0)
            residual_out[p, l] = value
            residual.append(value)
        g0, g1, g2 = residual
        back = (g0 + g1 * (2.0 * THIRD) + g2 * THIRD) + lane_roll(g1 * THIRD + g2 * (2.0 * THIRD), 1)
        back_high, back_low = halves(back)
        stacked = jnp.concatenate([back_high, back_low, back_high], axis=0)
        sums = lax.dot_general(gather, stacked, (((0,), (0,)), ((), ())), preferred_element_type=F32)
        back_out[4 * l : 4 * l + 4, :] = sums[2:6]
        lower_scr[at : at + 2, :] = sums[0:2]
        higher_scr[at : at + 2, :] = sums[6:8]
    same_start = jnp.where(parity == 0, own_fine - 2, 0)
    cross_start = jnp.where(parity == 0, 0, own_fine - 2)
    for p in range(3):
        for l in range(levels):
            at = (p * levels + l) * 2
            for k in range(2):
                same_out[at + k : at + k + 1, :] = residual_out[p, l, pl.ds(same_start + k, 1), :]
                cross_out[at + k : at + k + 1, :] = residual_out[p, l, pl.ds(cross_start + k, 1), :]
    lower, higher = lower_scr[...], higher_scr[...]
    same_out[3 * size : 4 * size, :] = jnp.where(parity == 0, higher, lower)
    cross_out[3 * size : 4 * size, :] = jnp.where(parity == 0, lower, higher)


def join_planes(planes):
    width = 128
    rows, count = planes[0].shape
    blocks = count // width
    spans = [slice(width * block, width * (block + 1)) for block in range(blocks)]
    joined = jnp.concatenate([jnp.concatenate([p[:, span] for p in planes], axis=1) for span in spans], axis=0)
    high, low = halves(joined)
    both = jnp.dot(jnp.concatenate([high, low], axis=0), triple_table(width, True), preferred_element_type=F32)
    mixed = both[: blocks * rows] + both[blocks * rows :]
    return [mixed[block * rows : (block + 1) * rows] for block in range(blocks)]


def own_gradient_kernel(scalars_ref, control_ref, residual_ref, out_ref, grad_scr):
    own_fine = scalars_ref[1, 0]
    planes, levels, slots, count = control_ref.shape
    row_ids = lax.broadcasted_iota(jnp.int32, (slots, 1), 0)
    exists = neighbours(scalars_ref)
    for l in range(levels):
        own = [residual_ref[p, l] for p in range(3)]
        first = [residual_ref[p, l, 0:1, :] for p in range(3)]
        last = [residual_ref[p, l, pl.ds(own_fine - 1, 1), :] for p in range(3)]
        result = spread_own(own, first, last, own_fine, row_ids, exists)
        for p in range(3):
            grad_scr[p, l] = jnp.where(row_ids < own_fine, control_ref[p, l] + result[p], 0.0)
    mixed = join_planes([grad_scr[p].reshape(levels * slots, count) for p in range(3)])
    for block, part in enumerate(mixed):
        out_ref[:, :, 384 * block : 384 * (block + 1)] = part.reshape(levels, slots, 384)


def gradient_kernel(
    scalars_ref, back_ref, cross_ref, same_ref, own_static_ref, alpha_ref, perturb_ref, loc_ref,
    alpha_out, static_out, full_scr, schur_scr, stage_scr, halo_scr, static_scr, sems,
):
    own_coarse, own_fine = scalars_ref[0, 0], scalars_ref[1, 0]
    members, levels, slots, count = perturb_ref.shape
    size = 2 * levels
    below, above = halo_rows(same_ref, cross_ref, scalars_ref, 3 * size, size)
    full_scr[...] = back_ref[...]
    for l in range(levels):
        full_scr[4 * l : 4 * l + 2, :] += below[2 * l : 2 * l + 2]
        for k in range(2):
            full_scr[pl.ds(4 * l + own_coarse - 2 + k, 1), :] += above[2 * l + k : 2 * l + k + 1]
    rows = members * levels * slots
    chunk = 256
    for c in range(count // chunk):
        span = slice(c * chunk, (c + 1) * chunk)
        perturb = perturb_ref[:, :, :, span].astype(F32).reshape(members, levels * slots, chunk)
        schur_scr[:, span] = (perturb * full_scr[:, span][None]).astype(BF16).reshape(rows, chunk)

    halos = [halo_rows(same_ref, cross_ref, scalars_ref, p * size, size) for p in range(3)]
    lower = spread_halo([h[0] for h in halos], 1)
    higher = spread_halo([h[1] for h in halos], 0)
    mixed = join_planes([jnp.concatenate([lower[p], higher[p]], axis=0) for p in range(3)])
    for block, part in enumerate(mixed):
        halo_scr[:, 384 * block : 384 * (block + 1)] = part
    static_scr[...] = own_static_ref[...]
    for l in range(levels):
        static_scr[l, 0:2, :] += halo_scr[2 * l : 2 * l + 2, :]
        for k in range(2):
            at = size + 2 * l + k
            static_scr[l, pl.ds(own_fine - 2 + k, 1), :] += halo_scr[at : at + 1, :]
    copies = [pltpu.make_async_copy(static_scr, static_out, sems.at[0])]
    copies[0].start()

    schur = schur_scr[...]
    live = (lax.broadcasted_iota(jnp.int32, (rows, 1), 0) % slots < own_coarse).astype(F32)
    for c in range(count // chunk):
        span = slice(c * chunk, (c + 1) * chunk)
        pulled = lax.dot_general(schur, loc_ref[span, :], (((1,), (1,)), ((), ())), preferred_element_type=F32)
        alpha = alpha_ref[:, :, :, span].astype(F32).reshape(rows, chunk)
        stage_scr[:, :, :, span] = ((alpha + pulled) * live).reshape(members, levels, slots, chunk).astype(BF16)
        copies.append(
            pltpu.make_async_copy(
                stage_scr.at[:, :, :, pl.ds(c * chunk, chunk)], alpha_out.at[:, :, :, pl.ds(c * chunk, chunk)], sems.at[1 + c]
            )
        )
        copies[-1].start()
    for copy in copies:
        copy.wait()


def on_device(
    perturb, alpha_control, loc_factor, static_control, innovation, obs_weight, coarse_rows, fine_rows, source_row, row_weight
):
    device = lax.axis_index("band").astype(jnp.int32).reshape(1, 1)
    members, levels, slots, count = perturb.shape
    fine_slots = static_control.shape[1]
    rows = levels * slots
    steps = count // 256

    partial = pl.pallas_call(
        localize_kernel,
        out_shape=jax.ShapeDtypeStruct((rows, count), F32),
        in_specs=[HBM] * 3,
        out_specs=VMEM,
        scratch_shapes=[
            pltpu.VMEM(alpha_control.shape, BF16),
            pltpu.VMEM(perturb.shape, BF16),
            pltpu.VMEM(loc_factor.shape, BF16),
            pltpu.SemaphoreType.DMA((2 + count // 512,)),
        ],
        compiler_params=params(61),
    )(alpha_control, perturb, loc_factor)
    peers = [mem_peer(partial, by) for by in (1, 3, 2)]

    plane = (3, levels, fine_slots, count)
    outgoing = jax.ShapeDtypeStruct((8 * levels, count), F32)
    wide = jax.ShapeDtypeStruct((6 * levels, count), F32)
    scalars, same_send, cross_send = pl.pallas_call(
        edges_kernel,
        out_shape=(jax.ShapeDtypeStruct((8, 128), jnp.int32), wide, wide),
        in_specs=[VMEM] * 4 + [HBM],
        out_specs=(VMEM,) * 3,
        compiler_params=params(24),
    )(device, coarse_rows.reshape(1, -1), fine_rows.reshape(1, -1), static_control, partial)
    static_from_cross = cross_chip(cross_send)
    static_from_same = same_chip(same_send)
    pair = jax.ShapeDtypeStruct((2 * levels, count), F32)
    total, same_send, cross_send = pl.pallas_call(
        increment_kernel,
        out_shape=(jax.ShapeDtypeStruct((rows, count), F32), pair, pair),
        in_specs=[VMEM] * 5,
        out_specs=(VMEM,) * 3,
        compiler_params=params(24),
    )(scalars, partial, *peers)
    from_cross = cross_chip(cross_send)
    from_same = same_chip(same_send)
    control, innovation_planes, weight_planes = pl.pallas_call(
        planes_kernel,
        out_shape=(
            jax.ShapeDtypeStruct(plane, F32), jax.ShapeDtypeStruct(plane, BF16), jax.ShapeDtypeStruct(plane, BF16)
        ),
        in_specs=[VMEM, HBM] + [VMEM] * 3,
        out_specs=(VMEM,) * 3,
        compiler_params=params(24),
    )(scalars, total, static_control, innovation, obs_weight)
    static_minus = pl.pallas_call(
        static_kernel,
        out_shape=jax.ShapeDtypeStruct(plane, F32),
        in_specs=[VMEM] * 5,
        out_specs=VMEM,
        compiler_params=params(24),
    )(scalars, static_from_cross, static_from_same, control, innovation_planes)

    residual, back, same_send, cross_send = pl.pallas_call(
        residual_kernel,
        out_shape=(jax.ShapeDtypeStruct(plane, F32), jax.ShapeDtypeStruct((rows, count), F32), outgoing, outgoing),
        in_specs=[VMEM] * 8,
        out_specs=(VMEM,) * 4,
        scratch_shapes=[pltpu.VMEM((2 * levels, count), F32), pltpu.VMEM((2 * levels, count), F32)],
        compiler_params=params(24),
    )(
        scalars, source_row.reshape(1, fine_slots), row_weight.reshape(1, fine_slots), total, from_cross, from_same,
        static_minus, weight_planes,
    )
    from_cross = cross_chip(cross_send)
    from_same = same_chip(same_send)

    own_static = pl.pallas_call(
        own_gradient_kernel,
        out_shape=jax.ShapeDtypeStruct(static_control.shape, F32),
        in_specs=[VMEM] * 3,
        out_specs=VMEM,
        scratch_shapes=[pltpu.VMEM(plane, F32)],
        compiler_params=params(24),
    )(scalars, control, residual)

    return pl.pallas_call(
        gradient_kernel,
        out_shape=(jax.ShapeDtypeStruct(perturb.shape, BF16), jax.ShapeDtypeStruct(static_control.shape, F32)),
        in_specs=[VMEM] * 8,
        out_specs=(HBM, HBM),
        scratch_shapes=[
            pltpu.VMEM((rows, count), F32),
            pltpu.VMEM((members * rows, count), BF16),
            pltpu.VMEM(perturb.shape, BF16),
            pltpu.VMEM((rows, 3 * count), F32),
            pltpu.VMEM(static_control.shape, F32),
            pltpu.SemaphoreType.DMA((1 + steps,)),
        ],
        compiler_params=params(24),
    )(scalars, back, from_cross, from_same, own_static, alpha_control, perturb, loc_factor)


def solution(mesh):
    placed = (
        P("mem", None, "band", None),
        P("mem", None, "band", None),
        P(),
        P(None, "band", None),
        P(None, "band", None),
        P(None, "band", None),
        P(),
        P(),
        P("band"),
        P("band"),
    )
    return jax.shard_map(
        on_device,
        mesh=mesh,
        in_specs=placed,
        out_specs=(P("mem", None, "band", None), P(None, "band", None)),
        check_vma=False,
    )
```

```python
import jax
import jax.numpy as jnp
from jax import lax
from jax.experimental import pallas as pl
from jax.experimental.pallas import tpu as pltpu
from jax.sharding import PartitionSpec as P

F32 = jnp.float32
BF16 = jnp.bfloat16
THIRD = 1.0 / 3.0
VMEM = pl.BlockSpec(memory_space=pltpu.VMEM)
HBM = pl.BlockSpec(memory_space=pltpu.HBM)


def params(mib):
    return pltpu.CompilerParams(vmem_limit_bytes=mib << 20)


def same_chip(x):
    peers = lax.axis_size("band")
    return lax.ppermute(x, "band", [(i, i ^ 1) for i in range(peers)])


def cross_chip(x):
    bands, mems = lax.axis_size("band"), lax.axis_size("mem")
    pairs = []
    for m in range(mems):
        pairs += [(i * mems + m, (i + 1) * mems + m) for i in range(1, bands - 1, 2)]
        pairs += [((i + 1) * mems + m, i * mems + m) for i in range(1, bands - 1, 2)]
        pairs += [(i * mems + m, i * mems + (m ^ 1)) for i in (0, bands - 1)]
    return lax.ppermute(x, ("band", "mem"), pairs)


def mem_peer(x, by):
    peers = lax.axis_size("mem")
    return lax.ppermute(x, "mem", [(i, (i + by) % peers) for i in range(peers)])


def triple_table(width, transposed):
    rows = lax.broadcasted_iota(jnp.int32, (3 * width, 3 * width), 0)
    cols = lax.broadcasted_iota(jnp.int32, (3 * width, 3 * width), 1)
    if transposed:
        rows, cols = cols, rows
    return (rows == 3 * (cols % width) + cols // width).astype(BF16)


def lane_roll(x, by):
    return pltpu.roll(x, by % x.shape[-1], x.ndim - 1)


def smooth(planes, north, south):
    f0, f1, f2 = planes
    west0 = lane_roll(f2, 1)
    east2 = lane_roll(f0, -1)
    common = f0 + f1
    tail = f1 + f2
    return (
        0.2 * (common + west0 + (north[0] + south[0])),
        0.2 * (common + f2 + (north[1] + south[1])),
        0.2 * (tail + east2 + (north[2] + south[2])),
    )


def spread_own(own, first, last, live, row_ids, exists):
    top = row_ids == 0
    bottom = row_ids == live - 1
    count = own[0].shape[0]

    def shifted(v, lower, upper):
        north = [jnp.where(top, lo, pltpu.roll(x, 1, 0)) for x, lo in zip(v, lower)]
        south = [jnp.where(bottom, up, pltpu.roll(x, count - 1, 0)) for x, up in zip(v, upper)]
        return north, south

    zero = [0.0] * 3
    once = smooth(own, *shifted(own, zero, zero))
    below = [f * (0.2 * exists[0]) for f in first]
    above = [f * (0.2 * exists[1]) for f in last]
    return smooth(once, *shifted(once, below, above))


def spread_halo(rows, nearest):
    pair = lax.broadcasted_iota(jnp.int32, (rows[0].shape[0], 1), 0) % 2
    touching = [pltpu.roll(r, (r.shape[0] - 1) if nearest == 1 else 1, 0) for r in rows]
    t0, t1, t2 = touching
    spreads = (t0 + t1 + lane_roll(t2, 1), t0 + t1 + t2, t1 + t2 + lane_roll(t0, -1))
    return [0.04 * jnp.where(pair == 1 - nearest, 2.0 * s + r, r) for s, r in zip(spreads, rows)]


def neighbours(scalars_ref):
    device, bands = scalars_ref[2, 0], scalars_ref[4, 0]
    return (device > 0).astype(F32), (device < bands - 1).astype(F32)


def halo_rows(same_ref, cross_ref, scalars_ref, at, size):
    parity = scalars_ref[3, 0]
    exists = neighbours(scalars_ref)
    same, cross = same_ref[at : at + size, :], cross_ref[at : at + size, :]
    return jnp.where(parity == 0, cross, same) * exists[0], jnp.where(parity == 0, same, cross) * exists[1]


def localize_kernel(alpha_ref, perturb_ref, loc_ref, out_ref, alpha_scr, perturb_scr, loc_scr, sems):
    members, levels, slots, count = alpha_ref.shape
    chunk = 512
    steps = count // chunk
    alpha_load = pltpu.make_async_copy(alpha_ref, alpha_scr, sems.at[0])
    perturb_load = pltpu.make_async_copy(perturb_ref, perturb_scr, sems.at[1])
    loads = []
    for c in range(steps):
        span = pl.ds(c * chunk, chunk)
        loads.append(pltpu.make_async_copy(loc_ref.at[:, span], loc_scr.at[:, span], sems.at[2 + c]))
    alpha_load.start()
    loads[0].start()
    loads[1].start()
    alpha_load.wait()
    perturb_load.start()
    alpha = alpha_scr[...].reshape(members * levels * slots, count)
    for c in range(steps):
        span = slice(c * chunk, (c + 1) * chunk)
        loads[c].wait()
        if c + 2 < steps:
            loads[c + 2].start()
        localized = jnp.dot(alpha, loc_scr[:, span], preferred_element_type=F32)
        if c == 0:
            perturb_load.wait()
        perturb = perturb_scr[:, :, :, span].astype(F32).reshape(members * levels * slots, chunk)
        out_ref[:, span] = jnp.sum((perturb * localized).reshape(members, levels * slots, chunk), axis=0)


def edges_kernel(device_ref, coarse_ref, fine_ref, control_ref, scalars_out, same_out, cross_out):
    bands = coarse_ref.shape[1]
    device = device_ref[0, 0]
    parity = device % 2
    band_ids = lax.broadcasted_iota(jnp.int32, (1, bands), 1)
    own_coarse = jnp.sum(jnp.where(band_ids == device, coarse_ref[...], 0))
    own_fine = jnp.sum(jnp.where(band_ids == device, fine_ref[...], 0))
    first_row = 3 * (device - parity) + parity * (6 - own_coarse)
    for i, value in enumerate((own_coarse, own_fine, device, parity, bands, first_row)):
        scalars_out[i : i + 1, :] = jnp.full((1, scalars_out.shape[1]), value, jnp.int32)
    levels, slots, count = control_ref.shape
    same_start = jnp.where(parity == 0, own_fine - 2, 0)
    cross_start = jnp.where(parity == 0, 0, own_fine - 2)
    take = lax.broadcasted_iota(jnp.int32, (8, slots), 0)
    slot = lax.broadcasted_iota(jnp.int32, (8, slots), 1)
    wanted = jnp.where(take < 2, same_start + take, cross_start + take - 2)
    pick = ((slot == wanted) & (take < 4)).astype(BF16)
    width = 128
    blocks = count // (3 * width)
    rows = [jnp.dot(pick, control_ref[l], preferred_element_type=F32) for l in range(levels)]
    stacked = [rows[l][:, 3 * width * i : 3 * width * (i + 1)] for i in range(blocks) for l in range(levels)]
    stacked = jnp.concatenate(stacked, axis=0).astype(BF16)
    planes = jnp.dot(stacked, triple_table(width, False), preferred_element_type=F32)
    for i in range(blocks):
        out = slice(width * i, width * (i + 1))
        for l in range(levels):
            at = (i * levels + l) * 8
            for p in range(3):
                to = (p * levels + l) * 2
                same_out[to : to + 2, out] = planes[at : at + 2, p * width : (p + 1) * width]
                cross_out[to : to + 2, out] = planes[at + 2 : at + 4, p * width : (p + 1) * width]


def planes_kernel(scalars_ref, after_ref, control_ref, innovation_ref, weight_ref, control_out, innovation_out, weight_out):
    own_fine = scalars_ref[1, 0]
    levels, slots, count = control_ref.shape
    width = 128
    rows = levels * slots
    live = (lax.broadcasted_iota(jnp.int32, (rows, 1), 0) % slots < own_fine).astype(F32)
    blocks = count // (3 * width)
    stacked = [
        r[:, :, 3 * width * i : 3 * width * (i + 1)].reshape(rows, 3 * width)
        for r in (control_ref, innovation_ref, weight_ref)
        for i in range(blocks)
    ]
    planes = jnp.dot(jnp.concatenate(stacked, axis=0), triple_table(width, False), preferred_element_type=F32)
    for i in range(blocks):
        out = slice(width * i, width * (i + 1))
        for p in range(3):
            control, innovation, weight = (
                planes[rows * (k * blocks + i) : rows * (k * blocks + i + 1), p * width : (p + 1) * width] for k in range(3)
            )
            control_out[p, :, :, out] = (control * live).reshape(levels, slots, width)
            innovation_out[p, :, :, out] = innovation.reshape(levels, slots, width).astype(BF16)
            weight_out[p, :, :, out] = (weight * live).reshape(levels, slots, width).astype(BF16)


def static_kernel(scalars_ref, cross_ref, same_ref, control_ref, innovation_ref, static_out):
    own_fine = scalars_ref[1, 0]
    planes, levels, slots, count = control_ref.shape
    size = 2 * levels
    row_ids = lax.broadcasted_iota(jnp.int32, (slots, 1), 0)
    exists = neighbours(scalars_ref)
    halos = [halo_rows(same_ref, cross_ref, scalars_ref, p * size, size) for p in range(3)]
    lower = spread_halo([h[0] for h in halos], 1)
    higher = spread_halo([h[1] for h in halos], 0)
    for l in range(levels):
        own = [control_ref[p, l] for p in range(3)]
        first = [control_ref[p, l, 0:1, :] for p in range(3)]
        last = [control_ref[p, l, pl.ds(own_fine - 1, 1), :] for p in range(3)]
        result = spread_own(own, first, last, own_fine, row_ids, exists)
        for p in range(3):
            static_out[p, l] = result[p] - innovation_ref[p, l].astype(F32)
            static_out[p, l, 0:2, :] += lower[p][2 * l : 2 * l + 2]
            for k in range(2):
                static_out[p, l, pl.ds(own_fine - 2 + k, 1), :] += higher[p][2 * l + k : 2 * l + k + 1]


def increment_kernel(scalars_ref, own_ref, a_ref, b_ref, c_ref, total_ref, same_out, cross_out):
    own_coarse, parity = scalars_ref[0, 0], scalars_ref[3, 0]
    total_ref[...] = (own_ref[...] + a_ref[...]) + (b_ref[...] + c_ref[...])
    levels = total_ref.shape[0] // 4
    same_start = jnp.where(parity == 0, own_coarse - 2, 0)
    cross_start = jnp.where(parity == 0, 0, own_coarse - 2)
    for l in range(levels):
        for k in range(2):
            row = 2 * l + k
            same_out[row : row + 1, :] = total_ref[pl.ds(4 * l + same_start + k, 1), :]
            cross_out[row : row + 1, :] = total_ref[pl.ds(4 * l + cross_start + k, 1), :]


def halves(x):
    high = x.astype(BF16)
    return high, (x - high.astype(F32)).astype(BF16)


def residual_kernel(
    scalars_ref, source_ref, upper_ref, total_ref, cross_ref, same_ref, static_ref, weight_ref,
    residual_out, back_out, same_out, cross_out, lower_scr, higher_scr,
):
    own_coarse, own_fine, device, parity, bands, first_row = (scalars_ref[i, 0] for i in range(6))
    planes, levels, slots, count = static_ref.shape
    size = 2 * levels
    row_ids = lax.broadcasted_iota(jnp.int32, (slots, 1), 0)
    picked = lax.broadcasted_iota(jnp.int32, (slots, slots), 0) == lax.broadcasted_iota(jnp.int32, (slots, slots), 1)
    source = jnp.sum(jnp.where(picked, source_ref[...], 0), axis=1, keepdims=True)
    upper = jnp.sum(jnp.where(picked, upper_ref[...], 0.0), axis=1, keepdims=True)
    live = (row_ids < own_fine).astype(F32)
    low_weight, high_weight = live * (1.0 - upper), live * upper
    latitudes = [first_row - 2, first_row - 1] + [first_row + s for s in range(4)]
    latitudes += [first_row + own_coarse, first_row + own_coarse + 1]
    usable = [device > 0] * 2 + [s < own_coarse for s in range(4)] + [device < bands - 1] * 2
    coefficients = [
        (jnp.where(source == lat, low_weight, 0.0) + jnp.where(source + 1 == lat, high_weight, 0.0)) * ok.astype(F32)
        for lat, ok in zip(latitudes, usable)
    ]
    high_part, low_part = halves(jnp.concatenate(coefficients, axis=1))
    gather = jnp.concatenate([high_part, high_part, low_part], axis=0)
    row_below, row_above = halo_rows(same_ref, cross_ref, scalars_ref, 0, size)
    for l in range(levels):
        at = 2 * l
        rows = [row_below[at : at + 1], row_below[at + 1 : at + 2]]
        rows += [total_ref[4 * l + s : 4 * l + s + 1, :] for s in range(4)]
        rows += [row_above[at : at + 1], row_above[at + 1 : at + 2]]
        band = coefficients[0] * rows[0]
        for c, r in zip(coefficients[1:], rows[1:]):
            band = band + c * r
        following = lane_roll(band, -1)
        fine = (band, (2.0 * band + following) * THIRD, (band + 2.0 * following) * THIRD)
        residual = []
        for p in range(3):
            value = weight_ref[p, l].astype(F32) * (fine[p] + static_ref[p, l])
            value = jnp.where(row_ids < own_fine, value, 0.0)
            residual_out[p, l] = value
            residual.append(value)
        g0, g1, g2 = residual
        back = (g0 + g1 * (2.0 * THIRD) + g2 * THIRD) + lane_roll(g1 * THIRD + g2 * (2.0 * THIRD), 1)
        back_high, back_low = halves(back)
        stacked = jnp.concatenate([back_high, back_low, back_high], axis=0)
        sums = lax.dot_general(gather, stacked, (((0,), (0,)), ((), ())), preferred_element_type=F32)
        back_out[4 * l : 4 * l + 4, :] = sums[2:6]
        lower_scr[at : at + 2, :] = sums[0:2]
        higher_scr[at : at + 2, :] = sums[6:8]
    same_start = jnp.where(parity == 0, own_fine - 2, 0)
    cross_start = jnp.where(parity == 0, 0, own_fine - 2)
    for p in range(3):
        for l in range(levels):
            at = (p * levels + l) * 2
            for k in range(2):
                same_out[at + k : at + k + 1, :] = residual_out[p, l, pl.ds(same_start + k, 1), :]
                cross_out[at + k : at + k + 1, :] = residual_out[p, l, pl.ds(cross_start + k, 1), :]
    lower, higher = lower_scr[...], higher_scr[...]
    same_out[3 * size : 4 * size, :] = jnp.where(parity == 0, higher, lower)
    cross_out[3 * size : 4 * size, :] = jnp.where(parity == 0, lower, higher)


def join_planes(planes):
    width = 128
    rows, count = planes[0].shape
    blocks = count // width
    spans = [slice(width * block, width * (block + 1)) for block in range(blocks)]
    joined = jnp.concatenate([jnp.concatenate([p[:, span] for p in planes], axis=1) for span in spans], axis=0)
    high, low = halves(joined)
    both = jnp.dot(jnp.concatenate([high, low], axis=0), triple_table(width, True), preferred_element_type=F32)
    mixed = both[: blocks * rows] + both[blocks * rows :]
    return [mixed[block * rows : (block + 1) * rows] for block in range(blocks)]


def own_gradient_kernel(scalars_ref, control_ref, residual_ref, out_ref, grad_scr):
    own_fine = scalars_ref[1, 0]
    planes, levels, slots, count = control_ref.shape
    row_ids = lax.broadcasted_iota(jnp.int32, (slots, 1), 0)
    exists = neighbours(scalars_ref)
    for l in range(levels):
        own = [residual_ref[p, l] for p in range(3)]
        first = [residual_ref[p, l, 0:1, :] for p in range(3)]
        last = [residual_ref[p, l, pl.ds(own_fine - 1, 1), :] for p in range(3)]
        result = spread_own(own, first, last, own_fine, row_ids, exists)
        for p in range(3):
            grad_scr[p, l] = jnp.where(row_ids < own_fine, control_ref[p, l] + result[p], 0.0)
    mixed = join_planes([grad_scr[p].reshape(levels * slots, count) for p in range(3)])
    for block, part in enumerate(mixed):
        out_ref[:, :, 384 * block : 384 * (block + 1)] = part.reshape(levels, slots, 384)


def gradient_kernel(
    scalars_ref, back_ref, cross_ref, same_ref, own_static_ref, alpha_ref, perturb_ref, loc_ref,
    alpha_out, static_out, full_scr, schur_scr, stage_scr, halo_scr, static_scr, sems,
):
    own_coarse, own_fine = scalars_ref[0, 0], scalars_ref[1, 0]
    members, levels, slots, count = perturb_ref.shape
    size = 2 * levels
    below, above = halo_rows(same_ref, cross_ref, scalars_ref, 3 * size, size)
    full_scr[...] = back_ref[...]
    for l in range(levels):
        full_scr[4 * l : 4 * l + 2, :] += below[2 * l : 2 * l + 2]
        for k in range(2):
            full_scr[pl.ds(4 * l + own_coarse - 2 + k, 1), :] += above[2 * l + k : 2 * l + k + 1]
    rows = members * levels * slots
    chunk = 256
    for c in range(count // chunk):
        span = slice(c * chunk, (c + 1) * chunk)
        perturb = perturb_ref[:, :, :, span].astype(F32).reshape(members, levels * slots, chunk)
        schur_scr[:, span] = (perturb * full_scr[:, span][None]).astype(BF16).reshape(rows, chunk)

    halos = [halo_rows(same_ref, cross_ref, scalars_ref, p * size, size) for p in range(3)]
    lower = spread_halo([h[0] for h in halos], 1)
    higher = spread_halo([h[1] for h in halos], 0)
    mixed = join_planes([jnp.concatenate([lower[p], higher[p]], axis=0) for p in range(3)])
    for block, part in enumerate(mixed):
        halo_scr[:, 384 * block : 384 * (block + 1)] = part
    static_scr[...] = own_static_ref[...]
    for l in range(levels):
        static_scr[l, 0:2, :] += halo_scr[2 * l : 2 * l + 2, :]
        for k in range(2):
            at = size + 2 * l + k
            static_scr[l, pl.ds(own_fine - 2 + k, 1), :] += halo_scr[at : at + 1, :]
    copies = [pltpu.make_async_copy(static_scr, static_out, sems.at[0])]
    copies[0].start()

    schur = schur_scr[...]
    live = (lax.broadcasted_iota(jnp.int32, (rows, 1), 0) % slots < own_coarse).astype(F32)
    for c in range(count // chunk):
        span = slice(c * chunk, (c + 1) * chunk)
        pulled = lax.dot_general(schur, loc_ref[span, :], (((1,), (1,)), ((), ())), preferred_element_type=F32)
        alpha = alpha_ref[:, :, :, span].astype(F32).reshape(rows, chunk)
        stage_scr[:, :, :, span] = ((alpha + pulled) * live).reshape(members, levels, slots, chunk).astype(BF16)
        copies.append(
            pltpu.make_async_copy(
                stage_scr.at[:, :, :, pl.ds(c * chunk, chunk)], alpha_out.at[:, :, :, pl.ds(c * chunk, chunk)], sems.at[1 + c]
            )
        )
        copies[-1].start()
    for copy in copies:
        copy.wait()


def on_device(
    perturb, alpha_control, loc_factor, static_control, innovation, obs_weight, coarse_rows, fine_rows, source_row, row_weight
):
    device = lax.axis_index("band").astype(jnp.int32).reshape(1, 1)
    members, levels, slots, count = perturb.shape
    fine_slots = static_control.shape[1]
    rows = levels * slots
    steps = count // 256

    partial = pl.pallas_call(
        localize_kernel,
        out_shape=jax.ShapeDtypeStruct((rows, count), F32),
        in_specs=[HBM] * 3,
        out_specs=VMEM,
        scratch_shapes=[
            pltpu.VMEM(alpha_control.shape, BF16),
            pltpu.VMEM(perturb.shape, BF16),
            pltpu.VMEM(loc_factor.shape, BF16),
            pltpu.SemaphoreType.DMA((2 + count // 512,)),
        ],
        compiler_params=params(53),
    )(alpha_control, perturb, loc_factor)
    peers = [mem_peer(partial, by) for by in (1, 3, 2)]

    plane = (3, levels, fine_slots, count)
    outgoing = jax.ShapeDtypeStruct((8 * levels, count), F32)
    device, partial = lax.optimization_barrier((device, partial))
    wide = jax.ShapeDtypeStruct((6 * levels, count), F32)
    scalars, same_send, cross_send = pl.pallas_call(
        edges_kernel,
        out_shape=(jax.ShapeDtypeStruct((8, 128), jnp.int32), wide, wide),
        in_specs=[VMEM] * 4,
        out_specs=(VMEM,) * 3,
        compiler_params=params(24),
    )(device, coarse_rows.reshape(1, -1), fine_rows.reshape(1, -1), static_control)
    static_from_cross = cross_chip(cross_send)
    static_from_same = same_chip(same_send)
    pair = jax.ShapeDtypeStruct((2 * levels, count), F32)
    total, same_send, cross_send = pl.pallas_call(
        increment_kernel,
        out_shape=(jax.ShapeDtypeStruct((rows, count), F32), pair, pair),
        in_specs=[VMEM] * 5,
        out_specs=(VMEM,) * 3,
        compiler_params=params(24),
    )(scalars, partial, *peers)
    from_cross = cross_chip(cross_send)
    from_same = same_chip(same_send)
    control, innovation_planes, weight_planes = pl.pallas_call(
        planes_kernel,
        out_shape=(
            jax.ShapeDtypeStruct(plane, F32), jax.ShapeDtypeStruct(plane, BF16), jax.ShapeDtypeStruct(plane, BF16)
        ),
        in_specs=[VMEM, HBM] + [VMEM] * 3,
        out_specs=(VMEM,) * 3,
        compiler_params=params(24),
    )(scalars, total, static_control, innovation, obs_weight)
    static_minus = pl.pallas_call(
        static_kernel,
        out_shape=jax.ShapeDtypeStruct(plane, F32),
        in_specs=[VMEM] * 5,
        out_specs=VMEM,
        compiler_params=params(24),
    )(scalars, static_from_cross, static_from_same, control, innovation_planes)

    residual, back, same_send, cross_send = pl.pallas_call(
        residual_kernel,
        out_shape=(jax.ShapeDtypeStruct(plane, F32), jax.ShapeDtypeStruct((rows, count), F32), outgoing, outgoing),
        in_specs=[VMEM] * 8,
        out_specs=(VMEM,) * 4,
        scratch_shapes=[pltpu.VMEM((2 * levels, count), F32), pltpu.VMEM((2 * levels, count), F32)],
        compiler_params=params(24),
    )(
        scalars, source_row.reshape(1, fine_slots), row_weight.reshape(1, fine_slots), total, from_cross, from_same,
        static_minus, weight_planes,
    )
    from_cross = cross_chip(cross_send)
    from_same = same_chip(same_send)

    own_static = pl.pallas_call(
        own_gradient_kernel,
        out_shape=jax.ShapeDtypeStruct(static_control.shape, F32),
        in_specs=[VMEM] * 3,
        out_specs=VMEM,
        scratch_shapes=[pltpu.VMEM(plane, F32)],
        compiler_params=params(24),
    )(scalars, control, residual)

    return pl.pallas_call(
        gradient_kernel,
        out_shape=(jax.ShapeDtypeStruct(perturb.shape, BF16), jax.ShapeDtypeStruct(static_control.shape, F32)),
        in_specs=[VMEM] * 8,
        out_specs=(HBM, HBM),
        scratch_shapes=[
            pltpu.VMEM((rows, count), F32),
            pltpu.VMEM((members * rows, count), BF16),
            pltpu.VMEM(perturb.shape, BF16),
            pltpu.VMEM((rows, 3 * count), F32),
            pltpu.VMEM(static_control.shape, F32),
            pltpu.SemaphoreType.DMA((1 + steps,)),
        ],
        compiler_params=params(24),
    )(scalars, back, from_cross, from_same, own_static, alpha_control, perturb, loc_factor)


def solution(mesh):
    placed = (
        P("mem", None, "band", None),
        P("mem", None, "band", None),
        P(),
        P(None, "band", None),
        P(None, "band", None),
        P(None, "band", None),
        P(),
        P(),
        P("band"),
        P("band"),
    )
    return jax.shard_map(
        on_device,
        mesh=mesh,
        in_specs=placed,
        out_specs=(P("mem", None, "band", None), P(None, "band", None)),
        check_vma=False,
    )
```

```python
import jax
import jax.numpy as jnp
from jax import lax
from jax.experimental import pallas as pl
from jax.experimental.pallas import tpu as pltpu
from jax.sharding import PartitionSpec as P

F32 = jnp.float32
BF16 = jnp.bfloat16
THIRD = 1.0 / 3.0
VMEM = pl.BlockSpec(memory_space=pltpu.VMEM)
HBM = pl.BlockSpec(memory_space=pltpu.HBM)


def params(mib):
    return pltpu.CompilerParams(vmem_limit_bytes=mib << 20)


def same_chip(x):
    peers = lax.axis_size("band")
    return lax.ppermute(x, "band", [(i, i ^ 1) for i in range(peers)])


def cross_chip(x):
    bands, mems = lax.axis_size("band"), lax.axis_size("mem")
    pairs = []
    for m in range(mems):
        pairs += [(i * mems + m, (i + 1) * mems + m) for i in range(1, bands - 1, 2)]
        pairs += [((i + 1) * mems + m, i * mems + m) for i in range(1, bands - 1, 2)]
        pairs += [(i * mems + m, i * mems + (m ^ 1)) for i in (0, bands - 1)]
    return lax.ppermute(x, ("band", "mem"), pairs)


def mem_peer(x, by):
    peers = lax.axis_size("mem")
    return lax.ppermute(x, "mem", [(i, (i + by) % peers) for i in range(peers)])


def triple_table(width, transposed):
    rows = lax.broadcasted_iota(jnp.int32, (3 * width, 3 * width), 0)
    cols = lax.broadcasted_iota(jnp.int32, (3 * width, 3 * width), 1)
    if transposed:
        rows, cols = cols, rows
    return (rows == 3 * (cols % width) + cols // width).astype(BF16)


def lane_roll(x, by):
    return pltpu.roll(x, by % x.shape[-1], x.ndim - 1)


def smooth(planes, north, south):
    f0, f1, f2 = planes
    west0 = lane_roll(f2, 1)
    east2 = lane_roll(f0, -1)
    common = f0 + f1
    tail = f1 + f2
    return (
        0.2 * (common + west0 + (north[0] + south[0])),
        0.2 * (common + f2 + (north[1] + south[1])),
        0.2 * (tail + east2 + (north[2] + south[2])),
    )


def spread_own(own, first, last, live, row_ids, exists):
    top = row_ids == 0
    bottom = row_ids == live - 1
    count = own[0].shape[0]

    def shifted(v, lower, upper):
        north = [jnp.where(top, lo, pltpu.roll(x, 1, 0)) for x, lo in zip(v, lower)]
        south = [jnp.where(bottom, up, pltpu.roll(x, count - 1, 0)) for x, up in zip(v, upper)]
        return north, south

    zero = [0.0] * 3
    once = smooth(own, *shifted(own, zero, zero))
    below = [f * (0.2 * exists[0]) for f in first]
    above = [f * (0.2 * exists[1]) for f in last]
    return smooth(once, *shifted(once, below, above))


def spread_halo(rows, nearest):
    pair = lax.broadcasted_iota(jnp.int32, (rows[0].shape[0], 1), 0) % 2
    touching = [pltpu.roll(r, (r.shape[0] - 1) if nearest == 1 else 1, 0) for r in rows]
    t0, t1, t2 = touching
    spreads = (t0 + t1 + lane_roll(t2, 1), t0 + t1 + t2, t1 + t2 + lane_roll(t0, -1))
    return [0.04 * jnp.where(pair == 1 - nearest, 2.0 * s + r, r) for s, r in zip(spreads, rows)]


def neighbours(scalars_ref):
    device, bands = scalars_ref[2, 0], scalars_ref[4, 0]
    return (device > 0).astype(F32), (device < bands - 1).astype(F32)


def halo_rows(same_ref, cross_ref, scalars_ref, at, size):
    parity = scalars_ref[3, 0]
    exists = neighbours(scalars_ref)
    same, cross = same_ref[at : at + size, :], cross_ref[at : at + size, :]
    return jnp.where(parity == 0, cross, same) * exists[0], jnp.where(parity == 0, same, cross) * exists[1]


def localize_kernel(alpha_ref, perturb_ref, loc_ref, out_ref, alpha_scr, perturb_scr, loc_scr, sems):
    members, levels, slots, count = alpha_ref.shape
    chunk = 512
    steps = count // chunk
    alpha_load = pltpu.make_async_copy(alpha_ref, alpha_scr, sems.at[0])
    perturb_load = pltpu.make_async_copy(perturb_ref, perturb_scr, sems.at[1])
    loads = []
    for c in range(steps):
        span = pl.ds(c * chunk, chunk)
        loads.append(pltpu.make_async_copy(loc_ref.at[:, span], loc_scr.at[:, span], sems.at[2 + c]))
    alpha_load.start()
    loads[0].start()
    loads[1].start()
    alpha_load.wait()
    perturb_load.start()
    alpha = alpha_scr[...].reshape(members * levels * slots, count)
    for c in range(steps):
        span = slice(c * chunk, (c + 1) * chunk)
        loads[c].wait()
        if c + 2 < steps:
            loads[c + 2].start()
        localized = jnp.dot(alpha, loc_scr[:, span], preferred_element_type=F32)
        if c == 0:
            perturb_load.wait()
        perturb = perturb_scr[:, :, :, span].astype(F32).reshape(members * levels * slots, chunk)
        out_ref[:, span] = jnp.sum((perturb * localized).reshape(members, levels * slots, chunk), axis=0)


def edges_kernel(device_ref, coarse_ref, fine_ref, control_ref, scalars_out, same_out, cross_out):
    bands = coarse_ref.shape[1]
    device = device_ref[0, 0]
    parity = device % 2
    band_ids = lax.broadcasted_iota(jnp.int32, (1, bands), 1)
    own_coarse = jnp.sum(jnp.where(band_ids == device, coarse_ref[...], 0))
    own_fine = jnp.sum(jnp.where(band_ids == device, fine_ref[...], 0))
    first_row = 3 * (device - parity) + parity * (6 - own_coarse)
    for i, value in enumerate((own_coarse, own_fine, device, parity, bands, first_row)):
        scalars_out[i : i + 1, :] = jnp.full((1, scalars_out.shape[1]), value, jnp.int32)
    levels, slots, count = control_ref.shape
    same_start = jnp.where(parity == 0, own_fine - 2, 0)
    cross_start = jnp.where(parity == 0, 0, own_fine - 2)
    take = lax.broadcasted_iota(jnp.int32, (8, slots), 0)
    slot = lax.broadcasted_iota(jnp.int32, (8, slots), 1)
    wanted = jnp.where(take < 2, same_start + take, cross_start + take - 2)
    pick = ((slot == wanted) & (take < 4)).astype(BF16)
    width = 128
    blocks = count // (3 * width)
    rows = [jnp.dot(pick, control_ref[l], preferred_element_type=F32) for l in range(levels)]
    stacked = [rows[l][:, 3 * width * i : 3 * width * (i + 1)] for i in range(blocks) for l in range(levels)]
    stacked = jnp.concatenate(stacked, axis=0).astype(BF16)
    planes = jnp.dot(stacked, triple_table(width, False), preferred_element_type=F32)
    for i in range(blocks):
        out = slice(width * i, width * (i + 1))
        for l in range(levels):
            at = (i * levels + l) * 8
            for p in range(3):
                to = (p * levels + l) * 2
                same_out[to : to + 2, out] = planes[at : at + 2, p * width : (p + 1) * width]
                cross_out[to : to + 2, out] = planes[at + 2 : at + 4, p * width : (p + 1) * width]


def static_kernel(
    scalars_ref, after_ref, cross_ref, same_ref, control_ref, innovation_ref, weight_ref,
    control_out, static_out, weight_out, innovation_scr,
):
    own_fine = scalars_ref[1, 0]
    levels, slots, count = control_ref.shape
    width = 128
    rows = levels * slots
    live = (lax.broadcasted_iota(jnp.int32, (rows, 1), 0) % slots < own_fine).astype(F32)
    blocks = count // (3 * width)
    stacked = [
        r[:, :, 3 * width * i : 3 * width * (i + 1)].reshape(rows, 3 * width)
        for r in (control_ref, innovation_ref, weight_ref)
        for i in range(blocks)
    ]
    planes = jnp.dot(jnp.concatenate(stacked, axis=0), triple_table(width, False), preferred_element_type=F32)
    for i in range(blocks):
        out = slice(width * i, width * (i + 1))
        for p in range(3):
            control, innovation, weight = (
                planes[rows * (k * blocks + i) : rows * (k * blocks + i + 1), p * width : (p + 1) * width] for k in range(3)
            )
            control_out[p, :, :, out] = (control * live).reshape(levels, slots, width)
            innovation_scr[p, :, :, out] = innovation.reshape(levels, slots, width)
            weight_out[p, :, :, out] = (weight * live).reshape(levels, slots, width).astype(BF16)
    size = 2 * levels
    row_ids = lax.broadcasted_iota(jnp.int32, (slots, 1), 0)
    exists = neighbours(scalars_ref)
    halos = [halo_rows(same_ref, cross_ref, scalars_ref, p * size, size) for p in range(3)]
    lower = spread_halo([h[0] for h in halos], 1)
    higher = spread_halo([h[1] for h in halos], 0)
    for l in range(levels):
        own = [control_out[p, l] for p in range(3)]
        first = [control_out[p, l, 0:1, :] for p in range(3)]
        last = [control_out[p, l, pl.ds(own_fine - 1, 1), :] for p in range(3)]
        result = spread_own(own, first, last, own_fine, row_ids, exists)
        for p in range(3):
            static_out[p, l] = result[p] - innovation_scr[p, l]
            static_out[p, l, 0:2, :] += lower[p][2 * l : 2 * l + 2]
            for k in range(2):
                static_out[p, l, pl.ds(own_fine - 2 + k, 1), :] += higher[p][2 * l + k : 2 * l + k + 1]


def increment_kernel(scalars_ref, own_ref, a_ref, b_ref, c_ref, total_ref, same_out, cross_out):
    own_coarse, parity = scalars_ref[0, 0], scalars_ref[3, 0]
    total_ref[...] = (own_ref[...] + a_ref[...]) + (b_ref[...] + c_ref[...])
    levels = total_ref.shape[0] // 4
    same_start = jnp.where(parity == 0, own_coarse - 2, 0)
    cross_start = jnp.where(parity == 0, 0, own_coarse - 2)
    for l in range(levels):
        for k in range(2):
            row = 2 * l + k
            same_out[row : row + 1, :] = total_ref[pl.ds(4 * l + same_start + k, 1), :]
            cross_out[row : row + 1, :] = total_ref[pl.ds(4 * l + cross_start + k, 1), :]


def halves(x):
    high = x.astype(BF16)
    return high, (x - high.astype(F32)).astype(BF16)


def residual_kernel(
    scalars_ref, source_ref, upper_ref, total_ref, cross_ref, same_ref, static_ref, weight_ref,
    residual_out, back_out, same_out, cross_out, lower_scr, higher_scr,
):
    own_coarse, own_fine, device, parity, bands, first_row = (scalars_ref[i, 0] for i in range(6))
    planes, levels, slots, count = static_ref.shape
    size = 2 * levels
    row_ids = lax.broadcasted_iota(jnp.int32, (slots, 1), 0)
    picked = lax.broadcasted_iota(jnp.int32, (slots, slots), 0) == lax.broadcasted_iota(jnp.int32, (slots, slots), 1)
    source = jnp.sum(jnp.where(picked, source_ref[...], 0), axis=1, keepdims=True)
    upper = jnp.sum(jnp.where(picked, upper_ref[...], 0.0), axis=1, keepdims=True)
    live = (row_ids < own_fine).astype(F32)
    low_weight, high_weight = live * (1.0 - upper), live * upper
    latitudes = [first_row - 2, first_row - 1] + [first_row + s for s in range(4)]
    latitudes += [first_row + own_coarse, first_row + own_coarse + 1]
    usable = [device > 0] * 2 + [s < own_coarse for s in range(4)] + [device < bands - 1] * 2
    coefficients = [
        (jnp.where(source == lat, low_weight, 0.0) + jnp.where(source + 1 == lat, high_weight, 0.0)) * ok.astype(F32)
        for lat, ok in zip(latitudes, usable)
    ]
    high_part, low_part = halves(jnp.concatenate(coefficients, axis=1))
    gather = jnp.concatenate([high_part, high_part, low_part], axis=0)
    row_below, row_above = halo_rows(same_ref, cross_ref, scalars_ref, 0, size)
    for l in range(levels):
        at = 2 * l
        rows = [row_below[at : at + 1], row_below[at + 1 : at + 2]]
        rows += [total_ref[4 * l + s : 4 * l + s + 1, :] for s in range(4)]
        rows += [row_above[at : at + 1], row_above[at + 1 : at + 2]]
        band = coefficients[0] * rows[0]
        for c, r in zip(coefficients[1:], rows[1:]):
            band = band + c * r
        following = lane_roll(band, -1)
        fine = (band, (2.0 * band + following) * THIRD, (band + 2.0 * following) * THIRD)
        residual = []
        for p in range(3):
            value = weight_ref[p, l].astype(F32) * (fine[p] + static_ref[p, l])
            value = jnp.where(row_ids < own_fine, value, 0.0)
            residual_out[p, l] = value
            residual.append(value)
        g0, g1, g2 = residual
        back = (g0 + g1 * (2.0 * THIRD) + g2 * THIRD) + lane_roll(g1 * THIRD + g2 * (2.0 * THIRD), 1)
        back_high, back_low = halves(back)
        stacked = jnp.concatenate([back_high, back_low, back_high], axis=0)
        sums = lax.dot_general(gather, stacked, (((0,), (0,)), ((), ())), preferred_element_type=F32)
        back_out[4 * l : 4 * l + 4, :] = sums[2:6]
        lower_scr[at : at + 2, :] = sums[0:2]
        higher_scr[at : at + 2, :] = sums[6:8]
    same_start = jnp.where(parity == 0, own_fine - 2, 0)
    cross_start = jnp.where(parity == 0, 0, own_fine - 2)
    for p in range(3):
        for l in range(levels):
            at = (p * levels + l) * 2
            for k in range(2):
                same_out[at + k : at + k + 1, :] = residual_out[p, l, pl.ds(same_start + k, 1), :]
                cross_out[at + k : at + k + 1, :] = residual_out[p, l, pl.ds(cross_start + k, 1), :]
    lower, higher = lower_scr[...], higher_scr[...]
    same_out[3 * size : 4 * size, :] = jnp.where(parity == 0, higher, lower)
    cross_out[3 * size : 4 * size, :] = jnp.where(parity == 0, lower, higher)


def join_planes(planes):
    width = 128
    rows, count = planes[0].shape
    blocks = count // width
    spans = [slice(width * block, width * (block + 1)) for block in range(blocks)]
    joined = jnp.concatenate([jnp.concatenate([p[:, span] for p in planes], axis=1) for span in spans], axis=0)
    high, low = halves(joined)
    both = jnp.dot(jnp.concatenate([high, low], axis=0), triple_table(width, True), preferred_element_type=F32)
    mixed = both[: blocks * rows] + both[blocks * rows :]
    return [mixed[block * rows : (block + 1) * rows] for block in range(blocks)]


def own_gradient_kernel(scalars_ref, control_ref, residual_ref, out_ref, grad_scr):
    own_fine = scalars_ref[1, 0]
    planes, levels, slots, count = control_ref.shape
    row_ids = lax.broadcasted_iota(jnp.int32, (slots, 1), 0)
    exists = neighbours(scalars_ref)
    for l in range(levels):
        own = [residual_ref[p, l] for p in range(3)]
        first = [residual_ref[p, l, 0:1, :] for p in range(3)]
        last = [residual_ref[p, l, pl.ds(own_fine - 1, 1), :] for p in range(3)]
        result = spread_own(own, first, last, own_fine, row_ids, exists)
        for p in range(3):
            grad_scr[p, l] = jnp.where(row_ids < own_fine, control_ref[p, l] + result[p], 0.0)
    mixed = join_planes([grad_scr[p].reshape(levels * slots, count) for p in range(3)])
    for block, part in enumerate(mixed):
        out_ref[:, :, 384 * block : 384 * (block + 1)] = part.reshape(levels, slots, 384)


def gradient_kernel(
    scalars_ref, back_ref, cross_ref, same_ref, own_static_ref, alpha_ref, perturb_ref, loc_ref,
    alpha_out, static_out, static_scr, full_scr, schur_scr, stage_scr, halo_scr, sems,
):
    own_coarse, own_fine = scalars_ref[0, 0], scalars_ref[1, 0]
    members, levels, slots, count = perturb_ref.shape
    size = 2 * levels
    below, above = halo_rows(same_ref, cross_ref, scalars_ref, 3 * size, size)
    full_scr[...] = back_ref[...]
    for l in range(levels):
        full_scr[4 * l : 4 * l + 2, :] += below[2 * l : 2 * l + 2]
        for k in range(2):
            full_scr[pl.ds(4 * l + own_coarse - 2 + k, 1), :] += above[2 * l + k : 2 * l + k + 1]
    rows = members * levels * slots
    chunk = 256
    for c in range(count // chunk):
        span = slice(c * chunk, (c + 1) * chunk)
        perturb = perturb_ref[:, :, :, span].astype(F32).reshape(members, levels * slots, chunk)
        schur_scr[:, span] = (perturb * full_scr[:, span][None]).astype(BF16).reshape(rows, chunk)

    halos = [halo_rows(same_ref, cross_ref, scalars_ref, p * size, size) for p in range(3)]
    lower = spread_halo([h[0] for h in halos], 1)
    higher = spread_halo([h[1] for h in halos], 0)
    mixed = join_planes([jnp.concatenate([lower[p], higher[p]], axis=0) for p in range(3)])
    for block, part in enumerate(mixed):
        halo_scr[:, 384 * block : 384 * (block + 1)] = part
    for l in range(levels):
        static_scr[l, 0:2, :] += halo_scr[2 * l : 2 * l + 2, :]
        for k in range(2):
            at = size + 2 * l + k
            static_scr[l, pl.ds(own_fine - 2 + k, 1), :] += halo_scr[at : at + 1, :]
    copies = [pltpu.make_async_copy(static_scr, static_out, sems.at[0])]
    copies[0].start()

    schur = schur_scr[...]
    live = (lax.broadcasted_iota(jnp.int32, (rows, 1), 0) % slots < own_coarse).astype(F32)
    for c in range(count // chunk):
        span = slice(c * chunk, (c + 1) * chunk)
        pulled = lax.dot_general(schur, loc_ref[span, :], (((1,), (1,)), ((), ())), preferred_element_type=F32)
        alpha = alpha_ref[:, :, :, span].astype(F32).reshape(rows, chunk)
        stage_scr[:, :, :, span] = ((alpha + pulled) * live).reshape(members, levels, slots, chunk).astype(BF16)
        copies.append(
            pltpu.make_async_copy(
                stage_scr.at[:, :, :, pl.ds(c * chunk, chunk)], alpha_out.at[:, :, :, pl.ds(c * chunk, chunk)], sems.at[1 + c]
            )
        )
        copies[-1].start()
    for copy in copies:
        copy.wait()


def on_device(
    perturb, alpha_control, loc_factor, static_control, innovation, obs_weight, coarse_rows, fine_rows, source_row, row_weight
):
    device = lax.axis_index("band").astype(jnp.int32).reshape(1, 1)
    members, levels, slots, count = perturb.shape
    fine_slots = static_control.shape[1]
    rows = levels * slots
    steps = count // 256

    partial = pl.pallas_call(
        localize_kernel,
        out_shape=jax.ShapeDtypeStruct((rows, count), F32),
        in_specs=[HBM] * 3,
        out_specs=VMEM,
        scratch_shapes=[
            pltpu.VMEM(alpha_control.shape, BF16),
            pltpu.VMEM(perturb.shape, BF16),
            pltpu.VMEM(loc_factor.shape, BF16),
            pltpu.SemaphoreType.DMA((2 + count // 512,)),
        ],
        compiler_params=params(53),
    )(alpha_control, perturb, loc_factor)
    peers = [mem_peer(partial, by) for by in (1, 3, 2)]

    plane = (3, levels, fine_slots, count)
    outgoing = jax.ShapeDtypeStruct((8 * levels, count), F32)
    device, partial = lax.optimization_barrier((device, partial))
    wide = jax.ShapeDtypeStruct((6 * levels, count), F32)
    scalars, same_send, cross_send = pl.pallas_call(
        edges_kernel,
        out_shape=(jax.ShapeDtypeStruct((8, 128), jnp.int32), wide, wide),
        in_specs=[VMEM] * 4,
        out_specs=(VMEM,) * 3,
        compiler_params=params(24),
    )(device, coarse_rows.reshape(1, -1), fine_rows.reshape(1, -1), static_control)
    static_from_cross = cross_chip(cross_send)
    static_from_same = same_chip(same_send)
    pair = jax.ShapeDtypeStruct((2 * levels, count), F32)
    total, same_send, cross_send = pl.pallas_call(
        increment_kernel,
        out_shape=(jax.ShapeDtypeStruct((rows, count), F32), pair, pair),
        in_specs=[VMEM] * 5,
        out_specs=(VMEM,) * 3,
        compiler_params=params(24),
    )(scalars, partial, *peers)
    from_cross = cross_chip(cross_send)
    from_same = same_chip(same_send)
    control, static_minus, weight_planes = pl.pallas_call(
        static_kernel,
        out_shape=(
            jax.ShapeDtypeStruct(plane, F32), jax.ShapeDtypeStruct(plane, F32), jax.ShapeDtypeStruct(plane, BF16)
        ),
        in_specs=[VMEM, HBM] + [VMEM] * 5,
        out_specs=(VMEM,) * 3,
        scratch_shapes=[pltpu.VMEM(plane, F32)],
        compiler_params=params(24),
    )(scalars, total, static_from_cross, static_from_same, static_control, innovation, obs_weight)

    residual, back, same_send, cross_send = pl.pallas_call(
        residual_kernel,
        out_shape=(jax.ShapeDtypeStruct(plane, F32), jax.ShapeDtypeStruct((rows, count), F32), outgoing, outgoing),
        in_specs=[VMEM] * 8,
        out_specs=(VMEM,) * 4,
        scratch_shapes=[pltpu.VMEM((2 * levels, count), F32), pltpu.VMEM((2 * levels, count), F32)],
        compiler_params=params(24),
    )(
        scalars, source_row.reshape(1, fine_slots), row_weight.reshape(1, fine_slots), total, from_cross, from_same,
        static_minus, weight_planes,
    )
    from_cross = cross_chip(cross_send)
    from_same = same_chip(same_send)

    own_static = pl.pallas_call(
        own_gradient_kernel,
        out_shape=jax.ShapeDtypeStruct(static_control.shape, F32),
        in_specs=[VMEM] * 3,
        out_specs=VMEM,
        scratch_shapes=[pltpu.VMEM(plane, F32)],
        compiler_params=params(24),
    )(scalars, control, residual)

    grad_alpha, grad_static, _ = pl.pallas_call(
        gradient_kernel,
        out_shape=(
            jax.ShapeDtypeStruct(perturb.shape, BF16),
            jax.ShapeDtypeStruct(static_control.shape, F32),
            jax.ShapeDtypeStruct(static_control.shape, F32),
        ),
        in_specs=[VMEM] * 8,
        out_specs=(HBM, HBM, VMEM),
        input_output_aliases={4: 2},
        scratch_shapes=[
            pltpu.VMEM((rows, count), F32),
            pltpu.VMEM((members * rows, count), BF16),
            pltpu.VMEM(perturb.shape, BF16),
            pltpu.VMEM((rows, 3 * count), F32),
            pltpu.SemaphoreType.DMA((1 + steps,)),
        ],
        compiler_params=params(24),
    )(scalars, back, from_cross, from_same, own_static, alpha_control, perturb, loc_factor)
    return grad_alpha, grad_static


def solution(mesh):
    placed = (
        P("mem", None, "band", None),
        P("mem", None, "band", None),
        P(),
        P(None, "band", None),
        P(None, "band", None),
        P(None, "band", None),
        P(),
        P(),
        P("band"),
        P("band"),
    )
    return jax.shard_map(
        on_device,
        mesh=mesh,
        in_specs=placed,
        out_specs=(P("mem", None, "band", None), P(None, "band", None)),
        check_vma=False,
    )
```
